32 devices in a mesh: groups: 2 (over y), seq: 16 (over z, x, core).
Axes of the slice: x: 2, y: 2, z: 4, core: 2. Of those that a mesh axis runs over, the one named last changes fastest.
Arguments:
- hidden_in: bfloat16 [2, 2048, 2048], P('groups', 'seq'), parts along dimension 0, may hold values from -6 to 6
- qkv: bfloat16 [2, 16, 2048, 384], P('groups', None, 'seq'), parts along dimension 0, may hold values from -6 to 6
- modulation: float32 [2, 4, 2048], P('groups'), parts along dimension 0, may hold values from -3 to 3
- route_weight: float32 [2, 2048, 2], P('groups', 'seq'), parts along dimension 0, may hold values from 0.2 to 1
- expert_ids: int32 [2, 2048, 2], P('groups', 'seq'), parts along dimension 0, may hold values from 0 to 15, as said below
- slots: int32 [2, 2048, 2], P('groups', 'seq'), parts along dimension 0, may hold values from 0 to 8, as said below
- w_in: bfloat16 [2048, 131072], P(None, 'seq'), may hold values from -0.125 to 0.125
- w_out: bfloat16 [131072, 2048], P('seq'), may hold values from -0.0625 to 0.0625
Outputs:
- block_out: bfloat16 [2, 2048, 2048], P('groups', 'seq'), parts along dimension 0
The draws below stay inside these ranges and needn't reach their ends.
There are 2 independent parts, one for each index of `groups`. The reference program is written for one: setup_inputs(seed, part) draws one part's arguments, and reference() takes and returns one part's arrays. A program takes and returns all parts, laid end to end along the dimension named above; an argument that names none is the same for every part. Nothing has to cross between parts.
Inputs may be any that keep to these rules, and one draw needn't show every extreme that they name: `expert_ids`: the two experts of a token differ. Within the rows of one device, the kept choices of each expert hold distinct slots 0, 1, ... upward, assigned in the device's priority order with all first choices before second choices; 8 marks a dropped choice.
All inputs are finite; a program needn't handle non-finite values.
Results may differ from the reference program's by a relative error of at most 0.0047.
Values may be sent and summed in bfloat16 or wider, within the bound.
No kernel may reach another device: no remote copies, remote signals or barrier semaphores. Data moves between devices by JAX's collectives and lax.ppermute only.
A program may use at most 192 MiB of HBM per device.

```python
import math
import jax
import jax.numpy as jnp
from jax import lax

HEADS = 16
HD = 128
D = 2048
EXPERTS = 16
FF = 8192
TOP = 2
CAP = 8
SEQS = 1
FRAMES = 16
TOK_DEV = 128
ROWS = 128
L = 2048
SHARDS = 1
FF_DEV = 8192


def route_table(key):
    blocks = L // ROWS
    key_hot, key_first, key_rank, key_second = jax.random.split(key, 4)
    hottest = jax.random.randint(key_hot, (blocks, 1), 0, EXPERTS)
    first_choice = jax.random.randint(key_first, (blocks, TOK_DEV), 0, EXPERTS)
    priority = jax.vmap(lambda one_key: jax.random.permutation(one_key, TOK_DEV))(jax.random.split(key_rank, blocks))
    first_choice = jnp.where(priority < 2 * CAP, hottest, first_choice)
    second_choice = (first_choice + 1 + jax.random.randint(key_second, (blocks, TOK_DEV), 0, EXPERTS - 1)) % EXPERTS
    chosen = jnp.stack([first_choice, second_choice], axis=-1).astype(jnp.int32)
    ordering = jnp.stack([priority, priority + TOK_DEV], axis=-1).reshape(blocks, 2 * TOK_DEV)
    flat = chosen.reshape(blocks, 2 * TOK_DEV)
    earlier = (flat[:, None, :] == flat[:, :, None]) & (ordering[:, None, :] < ordering[:, :, None])
    slot_assignment = jnp.minimum(jnp.sum(earlier.astype(jnp.int32), axis=-1), CAP).astype(jnp.int32)

    def arrange(array):
        return array.reshape(blocks, SEQS, ROWS, 2).transpose(1, 0, 2, 3).reshape(SEQS, L, 2)
    return (arrange(chosen), arrange(slot_assignment.reshape(blocks, TOK_DEV, 2)))


def draw_expert_ids(key, part):
    chosen, slot_assignment = route_table(key)
    return chosen


def draw_slots(key, part):
    chosen, slot_assignment = route_table(key)
    return slot_assignment


def draw_qkv(key, part):
    key = jax.random.fold_in(key, 11)
    key_base = jax.random.fold_in(key, 0)
    shape = (SEQS, HEADS, L, 3 * HD)
    column = jnp.arange(3 * HD)
    spread = jnp.where(column < 2 * HD, 1.6, 1.0).astype(jnp.float32)
    base = jnp.clip(jax.random.normal(key_base, shape, jnp.float32) * spread, -6.0, 6.0)
    return base.astype(jnp.bfloat16)


def steps_of(key, dims, shards, smallest, largest):
    def one(axis_at, parts):
        steps = jax.random.uniform(jax.random.fold_in(jax.random.fold_in(key, 6), axis_at), (parts,), jnp.float32, smallest / len(shards), largest / len(shards))
        return jnp.repeat(jnp.exp(steps), dims[axis_at] // parts).reshape((-1,) + (1,) * (len(dims) - axis_at - 1))

    factor_of = one(*shards[0])
    for cut in shards[1:]:
        factor_of = factor_of * one(*cut)
    return factor_of


def bell_draw(own_key, extent, scale, most, pieces=(), kind=jnp.bfloat16):
    gain = steps_of(own_key, extent, pieces, -0.22, 0.18) if pieces else 1.0
    entries = jax.random.normal(own_key, extent, jnp.float32) * scale * gain
    return jnp.minimum(jnp.maximum(entries, -most), most).astype(kind)


def setup_inputs(seed: int = 0, part: int = 0) -> dict:
    seeds = jax.random.split(jax.random.key(seed), 9)
    part_keys = jax.random.split(jax.random.fold_in(seeds[8], part), 9)
    return {
        "hidden_in": bell_draw(part_keys[0], (SEQS, L, D), 1.0, 6.0, ((1, 16),)),
        "qkv": draw_qkv(jax.random.fold_in(jax.random.fold_in(seeds[8], part), 71), part),
        "modulation": bell_draw(part_keys[2], (SEQS, 4, D), 0.7, 3.0, (), jnp.float32),
        "route_weight": jnp.clip(jnp.exp(math.log(1.0) - 1.609438 * jax.random.uniform(part_keys[3], (SEQS, L, TOP), jnp.float32) ** steps_of(part_keys[3], (SEQS, L, TOP), ((1, 16),), -0.2, 0.2)), 0.2, 1.0),
        "expert_ids": draw_expert_ids(jax.random.fold_in(jax.random.fold_in(seeds[8], part), 71), part),
        "slots": draw_slots(jax.random.fold_in(jax.random.fold_in(seeds[8], part), 71), part),
        "w_in": bell_draw(seeds[6], (D, EXPERTS * FF), D ** -0.5, 0.125, ((1, 16),)),
        "w_out": bell_draw(seeds[7], (EXPERTS * FF, D), FF ** -0.5, 0.0625, ((0, 16),)),
    }


def attend(queries, key_rows, values):
    length, width = queries.shape
    block_rows = math.gcd(length, 512)
    stacked = queries.reshape(length // block_rows, block_rows, width)

    def scores_for(query_block):
        scores = jnp.dot(query_block, key_rows.T, preferred_element_type=jnp.float32) * width ** (-0.5)
        scores = scores - lax.optimization_barrier(jnp.max(scores, axis=-1, keepdims=True))
        exponent = jnp.exp(scores)
        weights = (exponent / lax.optimization_barrier(jnp.sum(exponent, axis=-1, keepdims=True))).astype(jnp.bfloat16)
        return jnp.dot(weights, values, preferred_element_type=jnp.float32).astype(jnp.bfloat16)
    return lax.map(scores_for, stacked).reshape(length, width)

def normalize(resid):
    center = lax.optimization_barrier(jnp.mean(resid, axis=-1, keepdims=True))
    shifted = resid - center
    spread = lax.optimization_barrier(jnp.mean(shifted * shifted, axis=-1, keepdims=True))
    return shifted * lax.rsqrt(spread + 1e-06)

def expert_part(row_block, first_proj, second_proj):
    inner = jax.nn.gelu(jnp.dot(row_block, first_proj, preferred_element_type=jnp.float32), approximate=True).astype(jnp.bfloat16)
    return jnp.dot(inner, second_proj, preferred_element_type=jnp.float32).astype(jnp.bfloat16)

def reference(hidden_in, qkv, modulation, route_weight, expert_ids, slots, w_in, w_out):
    span = L // FRAMES
    heads_all = qkv.reshape(SEQS * HEADS, span, FRAMES, 3 * HD).transpose(0, 2, 1, 3).reshape(SEQS * HEADS * FRAMES, span, 3 * HD)
    attended = lax.map(lambda one_frame: attend(one_frame[:, :HD], one_frame[:, HD:2 * HD], one_frame[:, 2 * HD:]), heads_all)
    mixed = attended.reshape(SEQS, HEADS, FRAMES, span, HD).transpose(0, 3, 2, 1, 4).reshape(SEQS, L, D)
    resid = hidden_in.astype(jnp.float32) + modulation[:, 0][:, None, :] * mixed.astype(jnp.float32)
    normed = (normalize(resid) * (1.0 + modulation[:, 2][:, None, :]) + modulation[:, 1][:, None, :]).astype(jnp.bfloat16)
    blocks = L // ROWS

    def by_device(array):
        last = array.shape[-1]
        return array.reshape(SEQS, blocks, ROWS, last).transpose(1, 0, 2, 3).reshape(blocks, SEQS * ROWS, last)
    token_rows = by_device(normed)
    chosen = by_device(expert_ids)
    slot_assignment = by_device(slots)
    weight = by_device(route_weight)
    code = jnp.where(slot_assignment < CAP, chosen * CAP + slot_assignment, -1)
    column = jnp.arange(EXPERTS * CAP, dtype=jnp.int32)
    hits = code[:, :, :, None] == column
    selected_expert = lax.optimization_barrier(jnp.sum(hits, axis=2)).astype(jnp.float32)
    holding_area = jnp.einsum('xpu,xpw->xuw', selected_expert, token_rows.astype(jnp.float32)).astype(jnp.bfloat16)
    slab = holding_area.reshape(blocks, EXPERTS, CAP, D).transpose(1, 0, 2, 3).reshape(EXPERTS, blocks * CAP, D)

    def one_expert(inputs):
        expert, row_block = inputs
        first_all = lax.dynamic_slice_in_dim(w_in, expert * FF, FF, 1)
        second_all = lax.dynamic_slice_in_dim(w_out, expert * FF, FF, 0)
        summed = jnp.zeros((row_block.shape[0], D), jnp.float32)
        for shard in range(SHARDS):
            lower_edge = shard * FF_DEV
            summed = summed + expert_part(row_block, first_all[:, lower_edge:lower_edge + FF_DEV], second_all[lower_edge:lower_edge + FF_DEV]).astype(jnp.float32)
        return summed
    combined_outputs = lax.map(one_expert, (jnp.arange(EXPERTS, dtype=jnp.int32), slab))
    combined_outputs = combined_outputs.reshape(EXPERTS, blocks, CAP, D).transpose(1, 0, 2, 3).reshape(blocks, EXPERTS * CAP, D)
    expert_blending = lax.optimization_barrier(jnp.sum(jnp.where(hits, weight[:, :, :, None], 0.0), axis=2))
    expert_mixture_layer = jnp.einsum('osl,olz->osz', expert_blending, combined_outputs, precision=lax.Precision.HIGHEST)
    expert_mixture_layer = expert_mixture_layer.reshape(blocks, SEQS, ROWS, D).transpose(1, 0, 2, 3).reshape(SEQS, L, D)
    return (resid + modulation[:, 3][:, None, :] * expert_mixture_layer).astype(jnp.bfloat16)
```

```python
import functools

import jax
import jax.numpy as jnp
import numpy as np
from jax import lax
from jax.experimental import pallas as pl
from jax.experimental.pallas import tpu as pltpu
from jax.sharding import PartitionSpec as P

EXPERTS = 16
CAP = 8
FRAMES = 16
MIB = 2**20

VMEM = pl.BlockSpec(memory_space=pltpu.VMEM)
ANY = pl.BlockSpec(memory_space=pl.ANY)


def frame_order(chunk, places, local_frames):
    index = np.arange(chunk).reshape(-1, places, local_frames).transpose(2, 0, 1).reshape(chunk)
    return (index[:, None] == np.arange(chunk)[None, :]).astype(np.float32)


def attention_kernel(local_frames, chunk, order_ref, back_ref, rows_ref, out_ref, framed, attended):
    total, triple = rows_ref.shape
    width = triple // 3
    length = total // local_frames
    piece = chunk // local_frames
    order = order_ref[...]
    back = back_ref[...]
    for c in range(total // chunk):
        rows = jnp.dot(order, rows_ref[c * chunk : (c + 1) * chunk], preferred_element_type=jnp.float32)
        framed[:, c * piece : (c + 1) * piece, :] = rows.astype(jnp.bfloat16).reshape(
            local_frames, piece, triple
        )
    block = min(length, 256)
    for f in range(local_frames):
        keys = framed[f, :, width : 2 * width]
        values = framed[f, :, 2 * width :]
        for b in range(length // block):
            queries = framed[f, b * block : (b + 1) * block, :width]
            scores = lax.dot_general(
                queries, keys, (((1,), (1,)), ((), ())), preferred_element_type=jnp.float32
            ) * width ** (-0.5)
            exponent = jnp.exp(scores - jnp.max(scores, axis=-1, keepdims=True))
            weights = (exponent / jnp.sum(exponent, axis=-1, keepdims=True)).astype(jnp.bfloat16)
            attended[f, b * block : (b + 1) * block, :] = jnp.dot(
                weights, values, preferred_element_type=jnp.float32
            ).astype(jnp.bfloat16)
    for c in range(total // chunk):
        rows = attended[:, c * piece : (c + 1) * piece, :].reshape(chunk, width)
        out_ref[c * chunk : (c + 1) * chunk, :] = jnp.dot(
            back, rows, preferred_element_type=jnp.float32
        ).astype(jnp.bfloat16)


def attention(rows, places, local_frames):
    total, triple = rows.shape
    width = triple // 3
    chunk = min(total, 256)
    order = frame_order(chunk, places, local_frames)
    return pl.pallas_call(
        functools.partial(attention_kernel, local_frames, chunk),
        out_shape=jax.ShapeDtypeStruct((total, width), jnp.bfloat16),
        in_specs=[VMEM] * 3,
        out_specs=VMEM,
        scratch_shapes=[
            pltpu.VMEM((local_frames, total // local_frames, triple), jnp.bfloat16),
            pltpu.VMEM((local_frames, total // local_frames, width), jnp.bfloat16),
        ],
        compiler_params=pltpu.CompilerParams(vmem_limit_bytes=24 * MIB),
    )(jnp.asarray(order, jnp.bfloat16), jnp.asarray(order.T, jnp.bfloat16), rows)


def residual(hidden_ref, mixed_ref, modulation_ref):
    heads, _, width = mixed_ref.shape
    parts = []
    for h in range(heads):
        columns = slice(h * width, (h + 1) * width)
        parts.append(
            hidden_ref[:, columns].astype(jnp.float32)
            + modulation_ref[0:1, columns] * mixed_ref[h].astype(jnp.float32)
        )
    return jnp.concatenate(parts, axis=1)


def slot_code(ids_ref, slots_ref):
    return jnp.where(slots_ref[...] < CAP, ids_ref[...] * CAP + slots_ref[...], -1)


def dispatch_kernel(hidden_ref, mixed_ref, modulation_ref, ids_ref, slots_ref, out_ref):
    resid = residual(hidden_ref, mixed_ref, modulation_ref)
    shifted = resid - jnp.mean(resid, axis=-1, keepdims=True)
    spread = jnp.mean(shifted * shifted, axis=-1, keepdims=True)
    normed = (
        shifted * lax.rsqrt(spread + 1e-06) * (1.0 + modulation_ref[2:3, :]) + modulation_ref[1:2, :]
    ).astype(jnp.bfloat16)
    code = slot_code(ids_ref, slots_ref)
    row = lax.broadcasted_iota(jnp.int32, (EXPERTS * CAP, code.shape[1]), 0)
    chosen = jnp.zeros(row.shape, jnp.float32)
    for i in range(code.shape[0]):
        chosen = chosen + jnp.where(code[i : i + 1, :] == row, 1.0, 0.0)
    out_ref[...] = jnp.dot(
        chosen.astype(jnp.bfloat16), normed, preferred_element_type=jnp.float32
    ).astype(jnp.bfloat16)


def dispatch(hidden, mixed, modulation, ids, slots):
    return pl.pallas_call(
        dispatch_kernel,
        out_shape=jax.ShapeDtypeStruct((EXPERTS * CAP, hidden.shape[1]), jnp.bfloat16),
        in_specs=[VMEM] * 5,
        out_specs=VMEM,
        compiler_params=pltpu.CompilerParams(vmem_limit_bytes=24 * MIB),
    )(hidden, mixed, modulation, ids, slots)


def expert_kernel(blocks, depth, rows_ref, first_ref, second_hbm, out_ref, total, held, arrived):
    step_width = first_ref.shape[1] // blocks

    def fetch(block, place):
        return pltpu.make_async_copy(
            second_hbm.at[pl.ds(pl.multiple_of(block * step_width, step_width), step_width)],
            held.at[place],
            arrived.at[place],
        )

    for place in range(min(depth, blocks)):
        fetch(place, place).start()
    total[...] = jnp.zeros_like(total)

    def step(block, _):
        place = lax.rem(block, depth)
        columns = pl.ds(pl.multiple_of(block * step_width, step_width), step_width)
        inner = jnp.dot(rows_ref[...], first_ref[:, columns], preferred_element_type=jnp.float32)
        inner = jax.nn.gelu(inner, approximate=True).astype(jnp.bfloat16)
        fetch(block, place).wait()
        total[...] += jnp.dot(inner, held[place], preferred_element_type=jnp.float32)

        @pl.when(block + depth < blocks)
        def _():
            fetch(block + depth, place).start()

        return 0

    lax.fori_loop(0, blocks, step, 0)
    out_ref[...] = total[...].astype(jnp.bfloat16)


def expert(rows, first, second):
    count, width = rows.shape
    hidden = first.shape[1]
    step_width = min(hidden, 1024)
    blocks = hidden // step_width
    depth = min(blocks, 3)
    return pl.pallas_call(
        functools.partial(expert_kernel, blocks, depth),
        out_shape=jax.ShapeDtypeStruct((count, width), jnp.bfloat16),
        in_specs=[VMEM, VMEM, ANY],
        out_specs=VMEM,
        scratch_shapes=[
            pltpu.VMEM((count, width), jnp.float32),
            pltpu.VMEM((depth, step_width, width), jnp.bfloat16),
            pltpu.SemaphoreType.DMA((depth,)),
        ],
        compiler_params=pltpu.CompilerParams(vmem_limit_bytes=26 * MIB),
        cost_estimate=pl.CostEstimate(
            flops=4 * count * width * hidden, bytes_accessed=2 * width * hidden, transcendentals=count * hidden
        ),
    )(rows, pltpu.with_memory_space_constraint(first, pltpu.VMEM), second)


def combine_kernel(shards, hidden_ref, mixed_ref, modulation_ref, ids_ref, slots_ref, gate_ref, back_ref, out_ref):
    resid = residual(hidden_ref, mixed_ref, modulation_ref)
    code = slot_code(ids_ref, slots_ref)
    count = code.shape[1]
    row = lax.broadcasted_iota(jnp.int32, (EXPERTS * CAP * shards, count), 0)
    slot = row // (CAP * shards) * CAP + row % CAP
    blending = jnp.zeros(row.shape, jnp.float32)
    for i in range(code.shape[0]):
        blending = blending + jnp.where(code[i : i + 1, :] == slot, gate_ref[i : i + 1, :], 0.0)
    blending = blending.T
    parts = []
    for _ in range(3):
        part = blending.astype(jnp.bfloat16)
        parts.append(part)
        blending = blending - part.astype(jnp.float32)
    mixture = jnp.dot(jnp.concatenate(parts, axis=0), back_ref[...], preferred_element_type=jnp.float32)
    mixture = mixture[:count] + (mixture[count : 2 * count] + mixture[2 * count :])
    out_ref[...] = (resid + modulation_ref[3:4, :] * mixture).astype(jnp.bfloat16)


def combine(shards, hidden, mixed, modulation, ids, slots, gate, back):
    return pl.pallas_call(
        functools.partial(combine_kernel, shards),
        out_shape=jax.ShapeDtypeStruct(hidden.shape, jnp.bfloat16),
        in_specs=[VMEM] * 7,
        out_specs=VMEM,
        compiler_params=pltpu.CompilerParams(vmem_limit_bytes=24 * MIB),
    )(hidden, mixed, modulation, ids, slots, gate, back)


def body(hidden_in, qkv, modulation, route_weight, expert_ids, slots, w_in, w_out):
    seq_count, head_count, row_count, triple = qkv.shape
    assert seq_count == 1
    head_width = triple // 3
    width = head_count * head_width
    devices = lax.axis_size("seq")
    frame_parts = devices // head_count
    local_frames = FRAMES // frame_parts
    places = row_count // FRAMES
    shards = devices // EXPERTS
    outgoing = qkv.reshape(head_count, places, frame_parts, local_frames, triple)
    outgoing = outgoing.transpose(0, 2, 1, 3, 4).reshape(devices, places * local_frames, triple)
    owned = lax.all_to_all(outgoing, "seq", split_axis=0, concat_axis=0, tiled=True)
    attended = attention(owned.reshape(-1, triple), places, local_frames)
    returned = lax.all_to_all(
        attended.reshape(devices, places * local_frames, head_width), "seq", split_axis=0, concat_axis=0, tiled=True
    )
    mixed = returned.reshape(head_count, frame_parts, places, local_frames, head_width)
    mixed = mixed.transpose(0, 2, 1, 3, 4).reshape(head_count, row_count, head_width)
    hidden = hidden_in[0]
    scales = modulation[0]
    ids = expert_ids[0].T
    slot_rows = slots[0].T
    gate = route_weight[0].T
    gathered = dispatch(hidden, mixed, scales, ids, slot_rows)
    spread_rows = jnp.broadcast_to(
        gathered.reshape(EXPERTS, 1, CAP, width), (EXPERTS, shards, CAP, width)
    ).reshape(devices, CAP, width)
    arrived = lax.all_to_all(spread_rows, "seq", split_axis=0, concat_axis=0, tiled=True)
    computed = expert(arrived.reshape(devices * CAP, width), w_in, w_out)
    brought = lax.all_to_all(
        computed.reshape(devices, CAP, width), "seq", split_axis=0, concat_axis=0, tiled=True
    )
    final = combine(shards, hidden, mixed, scales, ids, slot_rows, gate, brought.reshape(devices * CAP, width))
    return final[None]


def solution(mesh):
    in_specs = (
        P("groups", "seq", None),
        P("groups", None, "seq", None),
        P("groups", None, None),
        P("groups", "seq", None),
        P("groups", "seq", None),
        P("groups", "seq", None),
        P(None, "seq"),
        P("seq", None),
    )
    out_specs = P("groups", "seq", None)
    return jax.shard_map(body, mesh=mesh, in_specs=in_specs, out_specs=out_specs, check_vma=False)
```

```python
import functools

import jax
import jax.numpy as jnp
from jax import lax
from jax.experimental import pallas as pl
from jax.experimental.pallas import tpu as pltpu
from jax.sharding import PartitionSpec as P

EXPERTS = 16
CAP = 8
FRAMES = 16
MIB = 2**20

VMEM = pl.BlockSpec(memory_space=pltpu.VMEM)
HBM = pl.BlockSpec(memory_space=pltpu.HBM)


def held(array):
    return pltpu.with_memory_space_constraint(array, pltpu.VMEM)


def frame_order(rows, transposed=False):
    places = rows // FRAMES
    out = lax.broadcasted_iota(jnp.int32, (rows, rows), 1 if transposed else 0)
    old = lax.broadcasted_iota(jnp.int32, (rows, rows), 0 if transposed else 1)
    return jnp.where(old == out % places * FRAMES + out // places, 1.0, 0.0).astype(jnp.bfloat16)


def prepare_kernel(
    shards, qkv_hbm, hidden_hbm, scales_hbm, ids_hbm, slots_hbm, gate_hbm,
    send_out, hidden_out, scales_out, chosen_out, blending_out, back_out,
    qkv, ids, slots, gate, done, qkv_done,
):
    heads = qkv.shape[0]
    copies = [
        pltpu.make_async_copy(source, target, done.at[i])
        for i, (source, target) in enumerate(
            ((ids_hbm, ids), (slots_hbm, slots), (gate_hbm, gate), (hidden_hbm, hidden_out), (scales_hbm, scales_out))
        )
    ]
    blocks = [pltpu.make_async_copy(qkv_hbm.at[h], qkv.at[h], qkv_done.at[h]) for h in range(heads)]
    for copy in blocks + copies:
        copy.start()
    order = frame_order(qkv.shape[1])
    back_out[...] = frame_order(qkv.shape[1], True)
    for h in range(heads):
        blocks[h].wait()
        send_out[h] = jnp.dot(order, qkv[h], preferred_element_type=jnp.float32).astype(jnp.bfloat16)
    for copy in copies:
        copy.wait()
    code = jnp.where(slots[...] < CAP, ids[...] * CAP + slots[...], -1)
    choices, count = code.shape
    row = lax.broadcasted_iota(jnp.int32, (EXPERTS * CAP, count), 0)
    chosen = jnp.zeros(row.shape, jnp.float32)
    for i in range(choices):
        chosen = chosen + jnp.where(code[i : i + 1, :] == row, 1.0, 0.0)
    chosen_out[...] = chosen.astype(jnp.bfloat16)
    row = lax.broadcasted_iota(jnp.int32, (EXPERTS * CAP * shards, count), 0)
    slot = row // (CAP * shards) * CAP + row % CAP
    blending = jnp.zeros(row.shape, jnp.float32)
    for i in range(choices):
        blending = blending + jnp.where(code[i : i + 1, :] == slot, gate[i : i + 1, :], 0.0)
    blending = blending.T
    for i in range(3):
        part = blending.astype(jnp.bfloat16)
        blending_out[i * count : (i + 1) * count, :] = part
        blending = blending - part.astype(jnp.float32)


def prepare(shards, qkv, hidden, scales, ids, slots, gate):
    count = ids.shape[1]
    slot_count = EXPERTS * CAP
    return pl.pallas_call(
        functools.partial(prepare_kernel, shards),
        out_shape=[
            jax.ShapeDtypeStruct(qkv.shape, qkv.dtype),
            pltpu.VMEM(hidden.shape, hidden.dtype),
            pltpu.VMEM(scales.shape, scales.dtype),
            pltpu.VMEM((slot_count, count), jnp.bfloat16),
            pltpu.VMEM((3 * count, slot_count * shards), jnp.bfloat16),
            pltpu.VMEM((count, count), jnp.bfloat16),
        ],
        in_specs=[HBM] * 6,
        out_specs=[VMEM] * 6,
        scratch_shapes=[
            pltpu.VMEM(qkv.shape, qkv.dtype),
            pltpu.VMEM(ids.shape, ids.dtype),
            pltpu.VMEM(slots.shape, slots.dtype),
            pltpu.VMEM(gate.shape, gate.dtype),
            pltpu.SemaphoreType.DMA((5,)),
            pltpu.SemaphoreType.DMA((qkv.shape[0],)),
        ],
        compiler_params=pltpu.CompilerParams(vmem_limit_bytes=24 * MIB),
    )(qkv, hidden, scales, ids, slots, gate)


def attention_kernel(places, rows_ref, out_ref):
    sources, rows, triple = rows_ref.shape
    width = triple // 3
    length = sources * places
    block = min(length, 256)
    pair = []
    for f in range(rows // places):
        frame = rows_ref[:, f * places : (f + 1) * places, :].astype(jnp.float32)
        frame = frame.reshape(length, triple).astype(jnp.bfloat16)
        keys = frame[:, width : 2 * width]
        values = frame[:, 2 * width :]
        attended = []
        for b in range(length // block):
            queries = frame[b * block : (b + 1) * block, :width]
            scores = lax.dot_general(
                queries, keys, (((1,), (1,)), ((), ())), preferred_element_type=jnp.float32
            ) * width ** (-0.5)
            exponent = jnp.exp(scores - jnp.max(scores, axis=-1, keepdims=True))
            weights = (exponent / jnp.sum(exponent, axis=-1, keepdims=True)).astype(jnp.bfloat16)
            attended.append(jnp.dot(weights, values, preferred_element_type=jnp.float32))
        pair.append(jnp.concatenate(attended, axis=0).reshape(sources, places, width))
        if len(pair) == 2:
            out_ref[:, (f - 1) * places : (f + 1) * places, :] = jnp.concatenate(pair, axis=1).astype(jnp.bfloat16)
            pair = []


def attention(rows, places):
    sources, count, triple = rows.shape
    return pl.pallas_call(
        functools.partial(attention_kernel, places),
        out_shape=jax.ShapeDtypeStruct((sources, count, triple // 3), jnp.bfloat16),
        in_specs=[VMEM],
        out_specs=VMEM,
        compiler_params=pltpu.CompilerParams(vmem_limit_bytes=32 * MIB),
    )(rows)


def residual(hidden_ref, mixed_ref, scales_ref, back_ref):
    heads = mixed_ref.shape[0]
    mixed = jnp.concatenate([mixed_ref[h] for h in range(heads)], axis=1)
    mixed = jnp.dot(back_ref[...], mixed, preferred_element_type=jnp.float32)
    return hidden_ref[...].astype(jnp.float32) + scales_ref[0:1, :] * mixed


def dispatch_kernel(hidden_ref, mixed_ref, scales_ref, back_ref, chosen_ref, out_ref):
    resid = residual(hidden_ref, mixed_ref, scales_ref, back_ref)
    shifted = resid - jnp.mean(resid, axis=-1, keepdims=True)
    spread = jnp.mean(shifted * shifted, axis=-1, keepdims=True)
    normed = (
        shifted * lax.rsqrt(spread + 1e-06) * (1.0 + scales_ref[2:3, :]) + scales_ref[1:2, :]
    ).astype(jnp.bfloat16)
    out_ref[...] = jnp.dot(chosen_ref[...], normed, preferred_element_type=jnp.float32).astype(jnp.bfloat16)


def dispatch(hidden, mixed, scales, back, chosen):
    return pl.pallas_call(
        dispatch_kernel,
        out_shape=jax.ShapeDtypeStruct((EXPERTS * CAP, hidden.shape[1]), jnp.bfloat16),
        in_specs=[VMEM] * 5,
        out_specs=VMEM,
        compiler_params=pltpu.CompilerParams(vmem_limit_bytes=24 * MIB),
    )(held(hidden), mixed, held(scales), held(back), held(chosen))


def expert_kernel(block, rows_ref, first_hbm, second_hbm, out_ref, total, first, second, first_done, second_done):
    blocks = first_hbm.shape[1] // block
    depth = first.shape[0]

    def fetch_first(step):
        place = lax.rem(step, depth)
        start = pl.multiple_of(step * block, block)
        return pltpu.make_async_copy(first_hbm.at[:, pl.ds(start, block)], first.at[place], first_done.at[place])

    def fetch_second(step):
        place = lax.rem(step, depth)
        start = pl.multiple_of(step * block, block)
        return pltpu.make_async_copy(second_hbm.at[pl.ds(start, block)], second.at[place], second_done.at[place])

    for step in range(min(depth, blocks)):
        fetch_first(step).start()
        fetch_second(step).start()
    total[...] = jnp.zeros_like(total)

    def work(step, _):
        place = lax.rem(step, depth)
        fetch_first(step).wait()
        inner = jnp.dot(rows_ref[...], first[place], preferred_element_type=jnp.float32)
        inner = jax.nn.gelu(inner, approximate=True).astype(jnp.bfloat16)

        @pl.when(step + depth < blocks)
        def _():
            fetch_first(step + depth).start()

        fetch_second(step).wait()
        total[...] += jnp.dot(inner, second[place], preferred_element_type=jnp.float32)

        @pl.when(step + depth < blocks)
        def _():
            fetch_second(step + depth).start()

        return 0

    lax.fori_loop(0, blocks, work, 0)
    out_ref[...] = total[...].astype(jnp.bfloat16)


def expert(rows, first, second):
    count, width = rows.shape
    hidden = first.shape[1]
    block = min(hidden, 1024)
    depth = min(hidden // block, 3)
    return pl.pallas_call(
        functools.partial(expert_kernel, block),
        out_shape=jax.ShapeDtypeStruct((count, width), jnp.bfloat16),
        in_specs=[VMEM, HBM, HBM],
        out_specs=VMEM,
        scratch_shapes=[
            pltpu.VMEM((count, width), jnp.float32),
            pltpu.VMEM((depth, width, block), jnp.bfloat16),
            pltpu.VMEM((depth, block, width), jnp.bfloat16),
            pltpu.SemaphoreType.DMA((depth,)),
            pltpu.SemaphoreType.DMA((depth,)),
        ],
        compiler_params=pltpu.CompilerParams(vmem_limit_bytes=44 * MIB),
        cost_estimate=pl.CostEstimate(
            flops=4 * count * width * hidden, bytes_accessed=4 * width * hidden, transcendentals=count * hidden
        ),
    )(rows, first, second)


def combine_kernel(hidden_ref, mixed_ref, scales_ref, back_ref, blending_ref, brought_ref, out_ref):
    resid = residual(hidden_ref, mixed_ref, scales_ref, back_ref)
    count = resid.shape[0]
    mixture = jnp.dot(blending_ref[...], brought_ref[...], preferred_element_type=jnp.float32)
    mixture = mixture[:count] + (mixture[count : 2 * count] + mixture[2 * count :])
    out_ref[...] = (resid + scales_ref[3:4, :] * mixture).astype(jnp.bfloat16)


def combine(hidden, mixed, scales, back, blending, brought):
    return pl.pallas_call(
        combine_kernel,
        out_shape=jax.ShapeDtypeStruct(hidden.shape, jnp.bfloat16),
        in_specs=[VMEM] * 6,
        out_specs=VMEM,
        compiler_params=pltpu.CompilerParams(vmem_limit_bytes=24 * MIB),
    )(held(hidden), mixed, held(scales), held(back), held(blending), brought)


def exchange(array):
    return lax.all_to_all(array, "seq", split_axis=0, concat_axis=0, tiled=True)


def body(hidden_in, qkv, modulation, route_weight, expert_ids, slots, w_in, w_out):
    seq_count, head_count, row_count, triple = qkv.shape
    assert seq_count == 1
    head_width = triple // 3
    width = head_count * head_width
    devices = lax.axis_size("seq")
    frame_parts = devices // head_count
    places = row_count // FRAMES
    shards = devices // EXPERTS
    send, hidden, scales, chosen, blending, back = prepare(
        shards, qkv[0], hidden_in[0], modulation[0], expert_ids[0].T, slots[0].T, route_weight[0].T
    )
    owned = exchange(send.reshape(devices, row_count // frame_parts, triple))
    returned = exchange(attention(owned, places))
    mixed = returned.reshape(head_count, row_count, head_width)
    gathered = dispatch(hidden, mixed, scales, back, chosen)
    spread_rows = jnp.broadcast_to(
        gathered.reshape(EXPERTS, 1, CAP, width), (EXPERTS, shards, CAP, width)
    ).reshape(devices, CAP, width)
    arrived = exchange(spread_rows)
    computed = expert(arrived.reshape(devices * CAP, width), w_in, w_out)
    brought = exchange(computed.reshape(devices, CAP, width))
    final = combine(hidden, mixed, scales, back, blending, brought.reshape(devices * CAP, width))
    return final[None]


def solution(mesh):
    in_specs = (
        P("groups", "seq", None),
        P("groups", None, "seq", None),
        P("groups", None, None),
        P("groups", "seq", None),
        P("groups", "seq", None),
        P("groups", "seq", None),
        P(None, "seq"),
        P("seq", None),
    )
    out_specs = P("groups", "seq", None)
    return jax.shard_map(body, mesh=mesh, in_specs=in_specs, out_specs=out_specs, check_vma=False)
```

```python
import functools
import math

import jax
import jax.numpy as jnp
from jax import lax
from jax.experimental import pallas as pl
from jax.experimental.pallas import tpu as pltpu
from jax.sharding import PartitionSpec as P

EXPERTS = 16
CAP = 8
FRAMES = 16
LAYER = 4
CODE_ROWS = 8
MIB = 2**20

VMEM = pl.BlockSpec(memory_space=pltpu.VMEM)
SMEM = pl.BlockSpec(memory_space=pltpu.SMEM)
HBM = pl.BlockSpec(memory_space=pltpu.HBM)


def held(array):
    return pltpu.with_memory_space_constraint(array, pltpu.VMEM)


def far(array):
    return pltpu.with_memory_space_constraint(array, pltpu.HBM)


def exchange(array):
    return lax.all_to_all(array, "seq", split_axis=0, concat_axis=0, tiled=True)


def slot_code(chosen, slot_assignment):
    return jnp.where(slot_assignment < CAP, chosen * CAP + slot_assignment, -1)


def one_hot(code, values=None, me=0):
    choices, count = code.shape
    row = lax.broadcasted_iota(jnp.int32, (EXPERTS * CAP, count), 0) ^ me * CAP
    hits = jnp.zeros(row.shape, jnp.float32)
    for i in range(choices):
        hits = hits + jnp.where(code[i : i + 1, :] == row, 1.0 if values is None else values[i : i + 1, :], 0.0)
    return hits


def frame_order(rows, transposed):
    each = rows // FRAMES
    out = lax.broadcasted_iota(jnp.int32, (rows, rows), 1 if transposed else 0)
    old = lax.broadcasted_iota(jnp.int32, (rows, rows), 0 if transposed else 1)
    return jnp.where(old == out % each * FRAMES + out // each, 1.0, 0.0).astype(jnp.bfloat16)


def prepare_kernel(
    me_ref, hidden_hbm, scales_hbm, ids_ref, slots_ref, gate_ref,
    scales_out, stay_out, core_out, chip_out, blending_out, hidden, done,
):
    copies = [
        pltpu.make_async_copy(hidden_hbm, hidden, done.at[0]),
        pltpu.make_async_copy(scales_hbm, scales_out, done.at[1]),
    ]
    for copy in copies:
        copy.start()
    code = slot_code(ids_ref[...], slots_ref[...])
    count = code.shape[1]
    blending = one_hot(code, gate_ref[...]).T
    for i in range(3):
        part = blending.astype(jnp.bfloat16)
        blending_out[i * count : (i + 1) * count, :] = part
        blending = blending - part.astype(jnp.float32)
    chosen = one_hot(code, me=me_ref[0]).astype(jnp.bfloat16)
    for copy in copies:
        copy.wait()
    layers, packed, lanes = stay_out.shape
    rows = jnp.dot(chosen, hidden[...], preferred_element_type=jnp.float32)
    for h in range(0, packed // CAP, 2):
        pair = [
            rows[:, (h + i) * lanes : (h + i + 1) * lanes].reshape(layers, LAYER, CAP, lanes) for i in range(2)
        ]
        pair = jnp.concatenate(pair, axis=2).astype(jnp.bfloat16)
        part = slice(h * CAP, (h + 2) * CAP)
        stay_out[:, part, :] = pair[:, 0]
        core_out[0, :, part, :] = pair[:, 1]
        chip_out[:, part, :] = pair[:, 2]
        core_out[1, :, part, :] = pair[:, 3]


def prepare(me, hidden, scales, ids, slots, gate, lanes):
    count, width = hidden.shape
    slot_count = EXPERTS * CAP
    layers = EXPERTS // LAYER
    block = (CAP * width // lanes, lanes)
    return pl.pallas_call(
        prepare_kernel,
        out_shape=[
            pltpu.VMEM(scales.shape, scales.dtype),
            jax.ShapeDtypeStruct((layers,) + block, hidden.dtype),
            jax.ShapeDtypeStruct((2, layers) + block, hidden.dtype),
            jax.ShapeDtypeStruct((layers,) + block, hidden.dtype),
            pltpu.VMEM((3 * count, slot_count), jnp.bfloat16),
        ],
        in_specs=[SMEM, HBM, HBM, VMEM, VMEM, VMEM],
        out_specs=[VMEM] * 5,
        scratch_shapes=[pltpu.VMEM(hidden.shape, hidden.dtype), pltpu.SemaphoreType.DMA((2,))],
        compiler_params=pltpu.CompilerParams(vmem_limit_bytes=16 * MIB),
        cost_estimate=pl.CostEstimate(flops=2 * slot_count * count * width, bytes_accessed=4 * MIB, transcendentals=0),
    )(me, far(hidden), far(scales), ids, slots, gate)


def regroup_kernel(*refs):
    sources, outs = refs[:LAYER], refs[LAYER:]
    for r, source in enumerate(sources):
        for i, out in enumerate(outs):
            out[r] = source[i + 1]


def regroup(*sources):
    layers, *block = sources[0].shape
    return pl.pallas_call(
        regroup_kernel,
        out_shape=[jax.ShapeDtypeStruct((LAYER, *block), sources[0].dtype)] * (layers - 1),
        in_specs=[VMEM] * LAYER,
        out_specs=[VMEM] * (layers - 1),
        compiler_params=pltpu.CompilerParams(vmem_limit_bytes=8 * MIB),
    )(*sources)


def assemble_kernel(me_ref, stay_ref, core_ref, chip_ref, both_ref, *refs):
    *layer_refs, out_ref = refs
    here = [stay_ref[0], core_ref[0, 0], chip_ref[0], both_ref[0]]
    for r in range(LAYER):
        out_ref[me_ref[0] ^ r] = here[r]
        for i, layer_ref in enumerate(layer_refs):
            out_ref[me_ref[0] ^ (LAYER * (i + 1) + r)] = layer_ref[r]


def assemble(me, stay, core, chip, both, layers):
    count = LAYER * (len(layers) + 1)
    return pl.pallas_call(
        assemble_kernel,
        out_shape=jax.ShapeDtypeStruct((count,) + stay.shape[1:], stay.dtype),
        in_specs=[SMEM] + [VMEM] * (4 + len(layers)),
        out_specs=VMEM,
        compiler_params=pltpu.CompilerParams(vmem_limit_bytes=8 * MIB),
    )(me, stay, core, chip, both, *layers)


def pack_kernel(qkv_hbm, ids_hbm, slots_hbm, send_ref, ids, slots, done):
    heads, count, triple = qkv_hbm.shape
    width = triple // 3
    copies = [
        pltpu.make_async_copy(ids_hbm, ids, done.at[0]),
        pltpu.make_async_copy(slots_hbm, slots, done.at[1]),
    ]
    copies += [
        pltpu.make_async_copy(
            qkv_hbm.at[:, :, pl.ds(i * width, width)], send_ref.at[:, pl.ds(i * count, count), :], done.at[2 + i]
        )
        for i in range(3)
    ]
    for copy in copies:
        copy.start()
    for copy in copies[:2]:
        copy.wait()
    own = slot_code(ids[...], slots[...]).astype(jnp.float32)
    own = jnp.concatenate([own, jnp.zeros((CODE_ROWS - own.shape[0], own.shape[1]), jnp.float32)])
    for h in range(heads):
        send_ref[h, 3 * count :, :] = own.astype(jnp.bfloat16)
    for copy in copies[2:]:
        copy.wait()


def pack(qkv, ids, slots):
    heads, count, triple = qkv.shape
    width = triple // 3
    return pl.pallas_call(
        pack_kernel,
        out_shape=pltpu.VMEM((heads, 3 * count + CODE_ROWS, width), qkv.dtype),
        in_specs=[HBM] * 3,
        out_specs=VMEM,
        scratch_shapes=[
            pltpu.VMEM(ids.shape, ids.dtype),
            pltpu.VMEM(slots.shape, slots.dtype),
            pltpu.SemaphoreType.DMA((5,)),
        ],
        compiler_params=pltpu.CompilerParams(vmem_limit_bytes=8 * MIB),
    )(far(qkv), far(ids), far(slots))


def attention_kernel(rows_ref, expert_out, attended_out, framed, attended):
    sources, packed, width = rows_ref.shape
    count = (packed - CODE_ROWS) // 3
    places = count // FRAMES
    piece = 2 * places
    order = frame_order(2 * count, False)
    for c in range(sources // 2):
        for i in range(3):
            rows = rows_ref[2 * c : 2 * c + 2, i * count : (i + 1) * count, :].reshape(2 * count, width)
            rows = jnp.dot(order, rows, preferred_element_type=jnp.float32)
            framed[i, :, c * piece : (c + 1) * piece, :] = rows.astype(jnp.bfloat16).reshape(FRAMES, piece, width)
    scores = lax.dot_general(
        framed[0], framed[1], (((2,), (2,)), ((0,), (0,))), preferred_element_type=jnp.float32
    ) * width ** (-0.5)
    exponent = jnp.exp(scores - jnp.max(scores, axis=-1, keepdims=True))
    weights = (exponent / jnp.sum(exponent, axis=-1, keepdims=True)).astype(jnp.bfloat16)
    result = lax.dot_general(weights, framed[2], (((2,), (1,)), ((0,), (0,))), preferred_element_type=jnp.float32)
    result = result.astype(jnp.bfloat16)
    attended_out[...] = result
    attended[...] = result.astype(jnp.float32)
    codes = rows_ref[:, 3 * count :, :].reshape(sources * CODE_ROWS, count)
    codes = lax.dot_general(
        codes, frame_order(count, False), (((1,), (1,)), ((), ())), preferred_element_type=jnp.float32
    )
    slot = lax.broadcasted_iota(jnp.int32, (EXPERTS * CAP, count), 0).astype(jnp.float32)
    for c in range(sources // 2):
        pair = []
        for s in (2 * c, 2 * c + 1):
            code = codes[s * CODE_ROWS : s * CODE_ROWS + 2]
            hit = (code[0:1] == slot) | (code[1:2] == slot)
            rows = attended[:, s * places : (s + 1) * places, :].reshape(count, width).astype(jnp.bfloat16)
            rows = jnp.dot(
                jnp.where(hit, 1.0, 0.0).astype(jnp.bfloat16), rows, preferred_element_type=jnp.float32
            )
            pair.append(rows.reshape(EXPERTS, CAP, width))
        expert_out[:, 2 * c * CAP : 2 * (c + 1) * CAP, :] = jnp.concatenate(pair, axis=1).astype(jnp.bfloat16)


def attention(rows):
    sources, packed, width = rows.shape
    by_frame = (FRAMES, sources * (packed - CODE_ROWS) // 3 // FRAMES, width)
    return pl.pallas_call(
        attention_kernel,
        out_shape=[
            jax.ShapeDtypeStruct((EXPERTS, sources * CAP, width), jnp.bfloat16),
            jax.ShapeDtypeStruct(by_frame, jnp.bfloat16),
        ],
        in_specs=[VMEM],
        out_specs=[VMEM] * 2,
        scratch_shapes=[pltpu.VMEM((3,) + by_frame, jnp.bfloat16), pltpu.VMEM(by_frame, jnp.float32)],
        compiler_params=pltpu.CompilerParams(vmem_limit_bytes=24 * MIB),
    )(rows)


def restore_kernel(attended_ref, out_ref):
    sources, count, width = out_ref.shape
    piece = 2 * count // FRAMES
    back = frame_order(2 * count, True)
    for c in range(sources // 2):
        rows = attended_ref[:, c * piece : (c + 1) * piece, :].reshape(2 * count, width)
        rows = jnp.dot(back, rows, preferred_element_type=jnp.float32).astype(jnp.bfloat16)
        out_ref[2 * c : 2 * c + 2] = rows.reshape(2, count, width)


def restore(attended, sources):
    frames, length, width = attended.shape
    return pl.pallas_call(
        restore_kernel,
        out_shape=jax.ShapeDtypeStruct((sources, frames * length // sources, width), attended.dtype),
        in_specs=[VMEM],
        out_specs=VMEM,
        compiler_params=pltpu.CompilerParams(vmem_limit_bytes=16 * MIB),
        cost_estimate=pl.CostEstimate(flops=2**35, bytes_accessed=MIB, transcendentals=0),
    )(attended)


def normalize(resid, scales_ref):
    shifted = resid - jnp.mean(resid, axis=-1, keepdims=True)
    spread = jnp.mean(shifted * shifted, axis=-1, keepdims=True)
    normed = shifted * lax.rsqrt(spread + 1e-06) * (1.0 + scales_ref[2:3, :]) + scales_ref[1:2, :]
    return normed.astype(jnp.bfloat16)


def expert_kernel(
    block, arrived_ref, hidden_ref, scales_ref, first_hbm, second_hbm, out_ref,
    rows, total, first, second, first_done, second_done,
):
    blocks = first_hbm.shape[1] // block
    depth = first.shape[0]

    def fetch_first(step):
        place = lax.rem(step, depth)
        start = pl.multiple_of(step * block, block)
        return pltpu.make_async_copy(first_hbm.at[:, pl.ds(start, block)], first.at[place], first_done.at[place])

    def fetch_second(step):
        place = lax.rem(step, depth)
        start = pl.multiple_of(step * block, block)
        return pltpu.make_async_copy(second_hbm.at[pl.ds(start, block)], second.at[place], second_done.at[place])

    for step in range(min(depth, blocks)):
        fetch_first(step).start()
        fetch_second(step).start()
    total[...] = jnp.zeros_like(total)
    heads, count, lanes = arrived_ref.shape
    parts = []
    for h in range(heads):
        columns = slice(h * lanes, (h + 1) * lanes)
        hidden = hidden_ref[:, h * CAP : (h + 1) * CAP, :].astype(jnp.float32)
        mixed = arrived_ref[h].astype(jnp.float32)
        parts.append(hidden.reshape(count, lanes) + scales_ref[0:1, columns] * mixed)
    rows[...] = normalize(jnp.concatenate(parts, axis=1), scales_ref)

    def work(step, _):
        place = lax.rem(step, depth)
        fetch_first(step).wait()
        inner = jnp.dot(rows[...], first[place], preferred_element_type=jnp.float32)
        inner = jax.nn.gelu(inner, approximate=True).astype(jnp.bfloat16)

        @pl.when(step + depth < blocks)
        def _():
            fetch_first(step + depth).start()

        fetch_second(step).wait()
        total[...] += jnp.dot(inner, second[place], preferred_element_type=jnp.float32)

        @pl.when(step + depth < blocks)
        def _():
            fetch_second(step + depth).start()

        return 0

    lax.fori_loop(0, blocks, work, 0)
    out_ref[...] = total[...].astype(jnp.bfloat16)


def expert(arrived, hidden_rows, scales, first, second):
    width, hidden = first.shape
    count = arrived.shape[0] * CAP
    block = math.gcd(hidden, 1024)
    depth = min(hidden // block, 3)
    return pl.pallas_call(
        functools.partial(expert_kernel, block),
        out_shape=jax.ShapeDtypeStruct((count, width), jnp.bfloat16),
        in_specs=[VMEM] * 3 + [HBM, HBM],
        out_specs=VMEM,
        scratch_shapes=[
            pltpu.VMEM((count, width), jnp.bfloat16),
            pltpu.VMEM((count, width), jnp.float32),
            pltpu.VMEM((depth, width, block), jnp.bfloat16),
            pltpu.VMEM((depth, block, width), jnp.bfloat16),
            pltpu.SemaphoreType.DMA((depth,)),
            pltpu.SemaphoreType.DMA((depth,)),
        ],
        compiler_params=pltpu.CompilerParams(vmem_limit_bytes=44 * MIB),
        cost_estimate=pl.CostEstimate(
            flops=64 * count * width * hidden, bytes_accessed=4 * width * hidden, transcendentals=count * hidden
        ),
    )(arrived, hidden_rows, held(scales), far(first), far(second))


def combine_kernel(hidden_ref, mixed_ref, scales_ref, blending_ref, brought_ref, out_ref):
    heads = mixed_ref.shape[0]
    mixed = jnp.concatenate([mixed_ref[h].astype(jnp.float32) for h in range(heads)], axis=1)
    resid = hidden_ref[...].astype(jnp.float32) + scales_ref[0:1, :] * mixed
    count = resid.shape[0]
    mixture = jnp.dot(blending_ref[...], brought_ref[...], preferred_element_type=jnp.float32)
    mixture = mixture[:count] + (mixture[count : 2 * count] + mixture[2 * count :])
    out_ref[...] = (resid + scales_ref[3:4, :] * mixture).astype(jnp.bfloat16)


def combine(hidden, mixed, scales, blending, brought):
    return pl.pallas_call(
        combine_kernel,
        out_shape=jax.ShapeDtypeStruct(hidden.shape, jnp.bfloat16),
        in_specs=[VMEM] * 5,
        out_specs=VMEM,
        compiler_params=pltpu.CompilerParams(vmem_limit_bytes=24 * MIB),
    )(hidden, mixed, held(scales), held(blending), brought)


def partner(array, step):
    devices = lax.axis_size("seq")
    return lax.ppermute(array, "seq", [(i, i ^ step) for i in range(devices)])


def direct_body(hidden_in, qkv, modulation, route_weight, expert_ids, slots, w_in, w_out):
    triple = qkv.shape[3]
    devices = lax.axis_size("seq")
    me = jnp.full((1,), lax.axis_index("seq"), jnp.int32)
    ids, slot_rows = expert_ids[0].T, slots[0].T
    owned = exchange(pack(qkv[0], ids, slot_rows))
    scales, stay, core, chip, blending = prepare(
        me, hidden_in[0], modulation[0], ids, slot_rows, route_weight[0].T, triple // 3
    )
    core = partner(core, 1)
    chip = partner(chip, 2)
    both = partner(core[1], 2)
    layers = regroup(stay, core[0], chip, both)
    *layers, owned = lax.optimization_barrier((*layers, owned))
    layers = [partner(layer, LAYER * (i + 1)) for i, layer in enumerate(layers)]
    to_experts, attended = attention(owned)
    arrived = exchange(to_experts)
    hidden_rows, attended = lax.optimization_barrier((assemble(me, stay, core, chip, both, layers), attended))
    to_places, arrived = lax.optimization_barrier((restore(attended, devices), arrived))
    mixed = exchange(to_places)
    computed = expert(arrived, hidden_rows, scales, w_in, w_out)
    mixed, computed = lax.optimization_barrier((mixed, computed))
    brought = exchange(computed.reshape(devices, CAP, -1))
    return combine(hidden_in[0], mixed, scales, blending, brought.reshape(devices * CAP, -1))[None]


def attend(queries, key_rows, values):
    length, width = queries.shape
    block_rows = math.gcd(length, 512)
    stacked = queries.reshape(length // block_rows, block_rows, width)

    def scores_for(query_block):
        scores = jnp.dot(query_block, key_rows.T, preferred_element_type=jnp.float32) * width ** (-0.5)
        scores = scores - jnp.max(scores, axis=-1, keepdims=True)
        exponent = jnp.exp(scores)
        weights = (exponent / jnp.sum(exponent, axis=-1, keepdims=True)).astype(jnp.bfloat16)
        return jnp.dot(weights, values, preferred_element_type=jnp.float32).astype(jnp.bfloat16)

    return lax.map(scores_for, stacked).reshape(length, width)


def split_body(hidden_in, qkv, modulation, route_weight, expert_ids, slots, w_in, w_out):
    seq_count, head_count, row_count, triple = qkv.shape
    head_width = triple // 3
    width = head_count * head_width
    devices_seq = lax.axis_size("seq")
    frame_parts = devices_seq // (seq_count * head_count)
    local_frames = FRAMES // frame_parts
    places = row_count // FRAMES
    arranged = qkv.reshape(seq_count, head_count, places, frame_parts, local_frames, triple)
    arranged = arranged.transpose(0, 1, 3, 2, 4, 5).reshape(devices_seq, places, local_frames, triple)
    owned = lax.all_to_all(arranged, "seq", split_axis=0, concat_axis=1, tiled=True)[0]
    by_frame = owned.transpose(1, 0, 2)
    attended = lax.map(
        lambda one_frame: attend(
            one_frame[:, :head_width],
            one_frame[:, head_width : 2 * head_width],
            one_frame[:, 2 * head_width :],
        ),
        by_frame,
    )
    outgoing = attended.transpose(1, 0, 2).reshape(devices_seq, places, local_frames, head_width)
    returned = exchange(outgoing)
    mixed = returned.reshape(seq_count, head_count, frame_parts, places, local_frames, head_width)
    mixed = mixed.transpose(0, 3, 2, 4, 1, 5).reshape(seq_count, row_count, width)
    resid = hidden_in.astype(jnp.float32) + modulation[:, 0][:, None, :] * mixed.astype(jnp.float32)
    center = jnp.mean(resid, axis=-1, keepdims=True)
    shifted = resid - center
    spread = jnp.mean(shifted * shifted, axis=-1, keepdims=True)
    normed = shifted * lax.rsqrt(spread + 1e-06)
    normed = (normed * (1.0 + modulation[:, 2][:, None, :]) + modulation[:, 1][:, None, :]).astype(jnp.bfloat16)
    token_rows = normed.reshape(seq_count * row_count, width)
    choice_count = expert_ids.shape[-1]
    code = slot_code(expert_ids, slots).reshape(-1, choice_count)
    weight = route_weight.reshape(-1, choice_count)
    hits = code[:, :, None] == jnp.arange(EXPERTS * CAP, dtype=jnp.int32)
    selected_expert = jnp.sum(hits, axis=1).astype(jnp.bfloat16)
    expert_blending = jnp.sum(jnp.where(hits, weight[:, :, None], 0.0), axis=1)
    gathered = jnp.einsum(
        "tk,td->kd", selected_expert, token_rows, preferred_element_type=jnp.float32
    ).astype(jnp.bfloat16)
    shards = devices_seq // EXPERTS
    spread_rows = jnp.broadcast_to(
        gathered.reshape(EXPERTS, 1, CAP, width), (EXPERTS, shards, CAP, width)
    ).reshape(devices_seq, CAP, width)
    arrived = exchange(spread_rows)
    inner = jax.nn.gelu(
        jnp.dot(arrived.reshape(-1, width), w_in, preferred_element_type=jnp.float32), approximate=True
    ).astype(jnp.bfloat16)
    computed = jnp.dot(inner, w_out, preferred_element_type=jnp.float32).astype(jnp.bfloat16)
    brought = exchange(computed.reshape(arrived.shape))
    combined_outputs = jnp.sum(
        brought.astype(jnp.float32).reshape(EXPERTS, shards, CAP, width), axis=1
    ).reshape(EXPERTS * CAP, width)
    mixture = jnp.dot(
        expert_blending, combined_outputs, precision=lax.Precision.HIGHEST, preferred_element_type=jnp.float32
    )
    final = resid + modulation[:, 3][:, None, :] * mixture.reshape(seq_count, row_count, width)
    return final.astype(jnp.bfloat16)


def body(*arrays):
    seq_count, head_count = arrays[1].shape[:2]
    devices = lax.axis_size("seq")
    if seq_count == 1 and devices == head_count == EXPERTS == 16:
        return direct_body(*arrays)
    return split_body(*arrays)


def solution(mesh):
    in_specs = (
        P("groups", "seq", None),
        P("groups", None, "seq", None),
        P("groups", None, None),
        P("groups", "seq", None),
        P("groups", "seq", None),
        P("groups", "seq", None),
        P(None, "seq"),
        P("seq", None),
    )
    out_specs = P("groups", "seq", None)
    return jax.shard_map(body, mesh=mesh, in_specs=in_specs, out_specs=out_specs, check_vma=False)
```

```python
import functools
import math

import jax
import jax.numpy as jnp
from jax import lax
from jax.experimental import pallas as pl
from jax.experimental.pallas import tpu as pltpu
from jax.sharding import PartitionSpec as P

EXPERTS = 16
CAP = 8
FRAMES = 16
LAYER = 4
CODE_ROWS = 8
MIB = 2**20

VMEM = pl.BlockSpec(memory_space=pltpu.VMEM)
SMEM = pl.BlockSpec(memory_space=pltpu.SMEM)
HBM = pl.BlockSpec(memory_space=pltpu.HBM)


def held(array):
    return pltpu.with_memory_space_constraint(array, pltpu.VMEM)


def far(array):
    return pltpu.with_memory_space_constraint(array, pltpu.HBM)


def exchange(array):
    return lax.all_to_all(array, "seq", split_axis=0, concat_axis=0, tiled=True)


def slot_code(chosen, slot_assignment):
    return jnp.where(slot_assignment < CAP, chosen * CAP + slot_assignment, -1)


def one_hot(code, values=None, me=0):
    choices, count = code.shape
    row = lax.broadcasted_iota(jnp.int32, (EXPERTS * CAP, count), 0) ^ me * CAP
    hits = jnp.zeros(row.shape, jnp.float32)
    for i in range(choices):
        hits = hits + jnp.where(code[i : i + 1, :] == row, 1.0 if values is None else values[i : i + 1, :], 0.0)
    return hits


def frame_order(rows, transposed):
    each = rows // FRAMES
    out = lax.broadcasted_iota(jnp.int32, (rows, rows), 1 if transposed else 0)
    old = lax.broadcasted_iota(jnp.int32, (rows, rows), 0 if transposed else 1)
    return jnp.where(old == out % each * FRAMES + out // each, 1.0, 0.0).astype(jnp.bfloat16)


def prepare_kernel(
    me_ref, hidden_hbm, scales_hbm, ids_ref, slots_ref, gate_ref,
    scales_out, stay_out, core_out, chip_out, blending_out, hidden, done,
):
    copies = [
        pltpu.make_async_copy(hidden_hbm, hidden, done.at[0]),
        pltpu.make_async_copy(scales_hbm, scales_out, done.at[1]),
    ]
    for copy in copies:
        copy.start()
    code = slot_code(ids_ref[...], slots_ref[...])
    count = code.shape[1]
    blending = one_hot(code, gate_ref[...]).T
    for i in range(3):
        part = blending.astype(jnp.bfloat16)
        blending_out[i * count : (i + 1) * count, :] = part
        blending = blending - part.astype(jnp.float32)
    chosen = one_hot(code, me=me_ref[0]).astype(jnp.bfloat16)
    for copy in copies:
        copy.wait()
    layers, packed, lanes = stay_out.shape
    rows = jnp.dot(chosen, hidden[...], preferred_element_type=jnp.float32)
    for h in range(0, packed // CAP, 2):
        pair = [
            rows[:, (h + i) * lanes : (h + i + 1) * lanes].reshape(layers, LAYER, CAP, lanes) for i in range(2)
        ]
        pair = jnp.concatenate(pair, axis=2).astype(jnp.bfloat16)
        part = slice(h * CAP, (h + 2) * CAP)
        stay_out[:, part, :] = pair[:, 0]
        core_out[0, :, part, :] = pair[:, 1]
        chip_out[:, part, :] = pair[:, 2]
        core_out[1, :, part, :] = pair[:, 3]


def prepare(me, hidden, scales, ids, slots, gate, lanes):
    count, width = hidden.shape
    slot_count = EXPERTS * CAP
    layers = EXPERTS // LAYER
    block = (CAP * width // lanes, lanes)
    return pl.pallas_call(
        prepare_kernel,
        out_shape=[
            pltpu.VMEM(scales.shape, scales.dtype),
            jax.ShapeDtypeStruct((layers,) + block, hidden.dtype),
            jax.ShapeDtypeStruct((2, layers) + block, hidden.dtype),
            jax.ShapeDtypeStruct((layers,) + block, hidden.dtype),
            pltpu.VMEM((3 * count, slot_count), jnp.bfloat16),
        ],
        in_specs=[SMEM, HBM, HBM, VMEM, VMEM, VMEM],
        out_specs=[VMEM] * 5,
        scratch_shapes=[pltpu.VMEM(hidden.shape, hidden.dtype), pltpu.SemaphoreType.DMA((2,))],
        compiler_params=pltpu.CompilerParams(vmem_limit_bytes=16 * MIB),
        cost_estimate=pl.CostEstimate(flops=2 * slot_count * count * width, bytes_accessed=4 * MIB, transcendentals=0),
    )(me, far(hidden), far(scales), ids, slots, gate)


def by_layer_kernel(*refs):
    for r in range(LAYER):
        for i in range(1, LAYER):
            refs[LAYER + i - 1][r] = refs[r][i]


def by_layer(*blocks):
    return pl.pallas_call(
        by_layer_kernel,
        out_shape=[jax.ShapeDtypeStruct(blocks[0].shape, blocks[0].dtype)] * (LAYER - 1),
        in_specs=[VMEM] * LAYER,
        out_specs=[VMEM] * (LAYER - 1),
        compiler_params=pltpu.CompilerParams(vmem_limit_bytes=8 * MIB),
    )(*blocks)


def by_place_kernel(*refs):
    stay_out, core_out, chip_out = refs[LAYER:]
    for i in range(LAYER):
        stay_out[i] = refs[i][0]
        core_out[0, i] = refs[i][1]
        chip_out[i] = refs[i][2]
        core_out[1, i] = refs[i][3]


def by_place(*blocks):
    shape = blocks[0].shape
    return pl.pallas_call(
        by_place_kernel,
        out_shape=[jax.ShapeDtypeStruct(shape, blocks[0].dtype) for shape in (shape, (2,) + shape, shape)],
        in_specs=[VMEM] * LAYER,
        out_specs=[VMEM] * 3,
        compiler_params=pltpu.CompilerParams(vmem_limit_bytes=8 * MIB),
    )(*blocks)


def assemble_kernel(me_ref, *refs):
    *block_refs, out_ref = refs
    here, away = block_refs[:LAYER], block_refs[LAYER:]
    for r in range(LAYER):
        for i in range(LAYER):
            out_ref[me_ref[0] ^ (LAYER * i + r)] = away[i - 1][r] if away and i else here[r][i]


def assemble(me, here, away=()):
    return pl.pallas_call(
        assemble_kernel,
        out_shape=jax.ShapeDtypeStruct((LAYER * LAYER,) + here[0].shape[1:], here[0].dtype),
        in_specs=[SMEM] + [VMEM] * (LAYER + len(away)),
        out_specs=VMEM,
        compiler_params=pltpu.CompilerParams(vmem_limit_bytes=8 * MIB),
    )(me, *here, *away)


def attention_kernel(me_ref, codes_ref, rows_ref, expert_out, attended_out, framed, attended, codes):
    sources, count, triple = rows_ref.shape
    width = triple // 3
    places = count // FRAMES
    piece = 2 * places
    order = frame_order(2 * count, False)
    for c in range(sources // 2):
        rows = rows_ref[2 * c : 2 * c + 2].reshape(2 * count, triple)
        rows = jnp.dot(order, rows, preferred_element_type=jnp.float32)
        framed[:, c * piece : (c + 1) * piece, :] = rows.astype(jnp.bfloat16).reshape(FRAMES, piece, triple)
    queries = framed[:, :, :width]
    keys = framed[:, :, width : 2 * width]
    values = framed[:, :, 2 * width :]
    scores = lax.dot_general(
        queries, keys, (((2,), (2,)), ((0,), (0,))), preferred_element_type=jnp.float32
    ) * width ** (-0.5)
    exponent = jnp.exp(scores - jnp.max(scores, axis=-1, keepdims=True))
    weights = (exponent / jnp.sum(exponent, axis=-1, keepdims=True)).astype(jnp.bfloat16)
    result = lax.dot_general(weights, values, (((2,), (1,)), ((0,), (0,))), preferred_element_type=jnp.float32)
    attended[...] = result.astype(jnp.bfloat16).astype(jnp.float32)
    codes[...] = jnp.zeros_like(codes)
    for s in range(sources):
        m = me_ref[0] ^ s
        codes[s * CODE_ROWS : s * CODE_ROWS + 2, :] = codes_ref[m // LAYER, m % LAYER].astype(jnp.float32)
    by_frame = lax.dot_general(
        codes[...].astype(jnp.bfloat16),
        frame_order(count, False),
        (((1,), (1,)), ((), ())),
        preferred_element_type=jnp.float32,
    )
    slot = lax.broadcasted_iota(jnp.int32, (EXPERTS * CAP, count), 0).astype(jnp.float32)
    for c in range(sources // 2):
        pair = []
        for s in (2 * c, 2 * c + 1):
            code = by_frame[s * CODE_ROWS : s * CODE_ROWS + 2]
            hit = (code[0:1] == slot) | (code[1:2] == slot)
            rows = attended[:, s * places : (s + 1) * places, :].reshape(count, width).astype(jnp.bfloat16)
            attended_out[s] = rows
            rows = jnp.dot(
                jnp.where(hit, 1.0, 0.0).astype(jnp.bfloat16), rows, preferred_element_type=jnp.float32
            )
            pair.append(rows.reshape(EXPERTS, CAP, width))
        expert_out[:, 2 * c * CAP : 2 * (c + 1) * CAP, :] = jnp.concatenate(pair, axis=1).astype(jnp.bfloat16)


def attention(me, codes, rows):
    sources, count, triple = rows.shape
    width = triple // 3
    by_frame = (FRAMES, sources * count // FRAMES)
    return pl.pallas_call(
        attention_kernel,
        out_shape=[
            jax.ShapeDtypeStruct((EXPERTS, sources * CAP, width), jnp.bfloat16),
            jax.ShapeDtypeStruct((sources, count, width), jnp.bfloat16),
        ],
        in_specs=[SMEM, VMEM, VMEM],
        out_specs=[VMEM] * 2,
        scratch_shapes=[
            pltpu.VMEM(by_frame + (triple,), jnp.bfloat16),
            pltpu.VMEM(by_frame + (width,), jnp.float32),
            pltpu.VMEM((sources * CODE_ROWS, count), jnp.float32),
        ],
        compiler_params=pltpu.CompilerParams(vmem_limit_bytes=24 * MIB),
    )(me, codes, rows)


def restore_kernel(me_ref, attended_ref, *outs):
    count = attended_ref.shape[1]
    back = frame_order(count, True)
    for m in range(LAYER * LAYER):
        rows = jnp.dot(back, attended_ref[me_ref[0] ^ m], preferred_element_type=jnp.float32)
        outs[m // LAYER][m % LAYER] = rows.astype(jnp.bfloat16)


def restore(me, attended):
    block = (LAYER,) + attended.shape[1:]
    return pl.pallas_call(
        restore_kernel,
        out_shape=[jax.ShapeDtypeStruct(block, attended.dtype)] * LAYER,
        in_specs=[SMEM, VMEM],
        out_specs=[VMEM] * LAYER,
        compiler_params=pltpu.CompilerParams(vmem_limit_bytes=16 * MIB),
        cost_estimate=pl.CostEstimate(flops=2**35, bytes_accessed=MIB, transcendentals=0),
    )(me, attended)


def normalize(resid, scales_ref):
    shifted = resid - jnp.mean(resid, axis=-1, keepdims=True)
    spread = jnp.mean(shifted * shifted, axis=-1, keepdims=True)
    normed = shifted * lax.rsqrt(spread + 1e-06) * (1.0 + scales_ref[2:3, :]) + scales_ref[1:2, :]
    return normed.astype(jnp.bfloat16)


def expert_kernel(
    block, arrived_ref, hidden_ref, scales_ref, first_hbm, second_hbm, out_ref,
    rows, total, first, second, first_done, second_done,
):
    blocks = first_hbm.shape[1] // block
    depth = first.shape[0]

    def fetch_first(step):
        place = lax.rem(step, depth)
        start = pl.multiple_of(step * block, block)
        return pltpu.make_async_copy(first_hbm.at[:, pl.ds(start, block)], first.at[place], first_done.at[place])

    def fetch_second(step):
        place = lax.rem(step, depth)
        start = pl.multiple_of(step * block, block)
        return pltpu.make_async_copy(second_hbm.at[pl.ds(start, block)], second.at[place], second_done.at[place])

    for step in range(min(depth, blocks)):
        fetch_first(step).start()
        fetch_second(step).start()
    total[...] = jnp.zeros_like(total)
    heads, count, lanes = arrived_ref.shape
    parts = []
    for h in range(heads):
        columns = slice(h * lanes, (h + 1) * lanes)
        hidden = hidden_ref[:, h * CAP : (h + 1) * CAP, :].astype(jnp.float32)
        mixed = arrived_ref[h].astype(jnp.float32)
        parts.append(hidden.reshape(count, lanes) + scales_ref[0:1, columns] * mixed)
    rows[...] = normalize(jnp.concatenate(parts, axis=1), scales_ref)

    def work(step, _):
        place = lax.rem(step, depth)
        fetch_first(step).wait()
        inner = jnp.dot(rows[...], first[place], preferred_element_type=jnp.float32)
        inner = jax.nn.gelu(inner, approximate=True).astype(jnp.bfloat16)

        @pl.when(step + depth < blocks)
        def _():
            fetch_first(step + depth).start()

        fetch_second(step).wait()
        total[...] += jnp.dot(inner, second[place], preferred_element_type=jnp.float32)

        @pl.when(step + depth < blocks)
        def _():
            fetch_second(step + depth).start()

        return 0

    lax.fori_loop(0, blocks, work, 0)
    out_ref[...] = total[...].astype(jnp.bfloat16)


def expert(arrived, hidden_rows, scales, first, second):
    width, hidden = first.shape
    count = arrived.shape[0] * CAP
    block = math.gcd(hidden, 1024)
    depth = min(hidden // block, 3)
    return pl.pallas_call(
        functools.partial(expert_kernel, block),
        out_shape=jax.ShapeDtypeStruct((count, width), jnp.bfloat16),
        in_specs=[VMEM] * 3 + [HBM, HBM],
        out_specs=VMEM,
        scratch_shapes=[
            pltpu.VMEM((count, width), jnp.bfloat16),
            pltpu.VMEM((count, width), jnp.float32),
            pltpu.VMEM((depth, width, block), jnp.bfloat16),
            pltpu.VMEM((depth, block, width), jnp.bfloat16),
            pltpu.SemaphoreType.DMA((depth,)),
            pltpu.SemaphoreType.DMA((depth,)),
        ],
        compiler_params=pltpu.CompilerParams(vmem_limit_bytes=44 * MIB),
        cost_estimate=pl.CostEstimate(
            flops=64 * count * width * hidden, bytes_accessed=4 * width * hidden, transcendentals=count * hidden
        ),
    )(arrived, hidden_rows, held(scales), far(first), far(second))


def combine_kernel(hidden_ref, mixed_ref, scales_ref, blending_ref, brought_ref, out_ref):
    heads = mixed_ref.shape[0]
    mixed = jnp.concatenate([mixed_ref[h].astype(jnp.float32) for h in range(heads)], axis=1)
    resid = hidden_ref[...].astype(jnp.float32) + scales_ref[0:1, :] * mixed
    count = resid.shape[0]
    mixture = jnp.dot(blending_ref[...], brought_ref[...], preferred_element_type=jnp.float32)
    mixture = mixture[:count] + (mixture[count : 2 * count] + mixture[2 * count :])
    out_ref[...] = (resid + scales_ref[3:4, :] * mixture).astype(jnp.bfloat16)


def combine(hidden, mixed, scales, blending, brought):
    return pl.pallas_call(
        combine_kernel,
        out_shape=jax.ShapeDtypeStruct(hidden.shape, jnp.bfloat16),
        in_specs=[VMEM] * 5,
        out_specs=VMEM,
        compiler_params=pltpu.CompilerParams(vmem_limit_bytes=24 * MIB),
    )(hidden, mixed, held(scales), held(blending), brought)


def partner(array, step):
    devices = lax.axis_size("seq")
    return lax.ppermute(array, "seq", [(i, i ^ step) for i in range(devices)])


def within_layer(stay, core, chip):
    core = partner(core, 1)
    chip = partner(chip, 2)
    return stay, core[0], chip, partner(core[1], 2)


def across_layers(blocks):
    return [partner(block, LAYER * (i + 1)) for i, block in enumerate(blocks)]


def gather_codes(code):
    layer = jnp.stack([code] + [partner(code, r) for r in range(1, LAYER)])
    return jnp.stack([layer] + [partner(layer, LAYER * i) for i in range(1, LAYER)])


def direct_body(hidden_in, qkv, modulation, route_weight, expert_ids, slots, w_in, w_out):
    triple = qkv.shape[3]
    devices = lax.axis_size("seq")
    me = jnp.full((1,), lax.axis_index("seq"), jnp.int32)
    ids, slot_rows = expert_ids[0].T, slots[0].T
    owned = exchange(qkv[0])
    codes = gather_codes(slot_code(ids, slot_rows))
    scales, stay, core, chip, blending = prepare(
        me, hidden_in[0], modulation[0], ids, slot_rows, route_weight[0].T, triple // 3
    )
    here = within_layer(stay, core, chip)
    near, *away = by_layer(*here)
    near, *away, owned = lax.optimization_barrier((partner(near, LAYER), *away, owned))
    away = [near, partner(away[0], 2 * LAYER), partner(away[1], 3 * LAYER)]
    to_experts, attended = attention(me, codes, owned)
    arrived = exchange(to_experts)
    hidden_rows, attended = lax.optimization_barrier((assemble(me, here, away), attended))
    here, *away = restore(me, attended)
    *away, arrived = lax.optimization_barrier((*away, arrived))
    away = across_layers(away)
    computed = expert(arrived, hidden_rows, scales, w_in, w_out)
    *away, computed = lax.optimization_barrier((*away, computed))
    brought = exchange(computed.reshape(devices, CAP, -1))
    mixed = assemble(me, within_layer(*by_place(here, *away)))
    return combine(hidden_in[0], mixed, scales, blending, brought.reshape(devices * CAP, -1))[None]


def attend(queries, key_rows, values):
    length, width = queries.shape
    block_rows = math.gcd(length, 512)
    stacked = queries.reshape(length // block_rows, block_rows, width)

    def scores_for(query_block):
        scores = jnp.dot(query_block, key_rows.T, preferred_element_type=jnp.float32) * width ** (-0.5)
        scores = scores - jnp.max(scores, axis=-1, keepdims=True)
        exponent = jnp.exp(scores)
        weights = (exponent / jnp.sum(exponent, axis=-1, keepdims=True)).astype(jnp.bfloat16)
        return jnp.dot(weights, values, preferred_element_type=jnp.float32).astype(jnp.bfloat16)

    return lax.map(scores_for, stacked).reshape(length, width)


def split_body(hidden_in, qkv, modulation, route_weight, expert_ids, slots, w_in, w_out):
    seq_count, head_count, row_count, triple = qkv.shape
    head_width = triple // 3
    width = head_count * head_width
    devices_seq = lax.axis_size("seq")
    frame_parts = devices_seq // (seq_count * head_count)
    local_frames = FRAMES // frame_parts
    places = row_count // FRAMES
    arranged = qkv.reshape(seq_count, head_count, places, frame_parts, local_frames, triple)
    arranged = arranged.transpose(0, 1, 3, 2, 4, 5).reshape(devices_seq, places, local_frames, triple)
    owned = lax.all_to_all(arranged, "seq", split_axis=0, concat_axis=1, tiled=True)[0]
    by_frame = owned.transpose(1, 0, 2)
    attended = lax.map(
        lambda one_frame: attend(
            one_frame[:, :head_width],
            one_frame[:, head_width : 2 * head_width],
            one_frame[:, 2 * head_width :],
        ),
        by_frame,
    )
    outgoing = attended.transpose(1, 0, 2).reshape(devices_seq, places, local_frames, head_width)
    returned = exchange(outgoing)
    mixed = returned.reshape(seq_count, head_count, frame_parts, places, local_frames, head_width)
    mixed = mixed.transpose(0, 3, 2, 4, 1, 5).reshape(seq_count, row_count, width)
    resid = hidden_in.astype(jnp.float32) + modulation[:, 0][:, None, :] * mixed.astype(jnp.float32)
    center = jnp.mean(resid, axis=-1, keepdims=True)
    shifted = resid - center
    spread = jnp.mean(shifted * shifted, axis=-1, keepdims=True)
    normed = shifted * lax.rsqrt(spread + 1e-06)
    normed = (normed * (1.0 + modulation[:, 2][:, None, :]) + modulation[:, 1][:, None, :]).astype(jnp.bfloat16)
    token_rows = normed.reshape(seq_count * row_count, width)
    choice_count = expert_ids.shape[-1]
    code = slot_code(expert_ids, slots).reshape(-1, choice_count)
    weight = route_weight.reshape(-1, choice_count)
    hits = code[:, :, None] == jnp.arange(EXPERTS * CAP, dtype=jnp.int32)
    selected_expert = jnp.sum(hits, axis=1).astype(jnp.bfloat16)
    expert_blending = jnp.sum(jnp.where(hits, weight[:, :, None], 0.0), axis=1)
    gathered = jnp.einsum(
        "tk,td->kd", selected_expert, token_rows, preferred_element_type=jnp.float32
    ).astype(jnp.bfloat16)
    shards = devices_seq // EXPERTS
    spread_rows = jnp.broadcast_to(
        gathered.reshape(EXPERTS, 1, CAP, width), (EXPERTS, shards, CAP, width)
    ).reshape(devices_seq, CAP, width)
    arrived = exchange(spread_rows)
    inner = jax.nn.gelu(
        jnp.dot(arrived.reshape(-1, width), w_in, preferred_element_type=jnp.float32), approximate=True
    ).astype(jnp.bfloat16)
    computed = jnp.dot(inner, w_out, preferred_element_type=jnp.float32).astype(jnp.bfloat16)
    brought = exchange(computed.reshape(arrived.shape))
    combined_outputs = jnp.sum(
        brought.astype(jnp.float32).reshape(EXPERTS, shards, CAP, width), axis=1
    ).reshape(EXPERTS * CAP, width)
    mixture = jnp.dot(
        expert_blending, combined_outputs, precision=lax.Precision.HIGHEST, preferred_element_type=jnp.float32
    )
    final = resid + modulation[:, 3][:, None, :] * mixture.reshape(seq_count, row_count, width)
    return final.astype(jnp.bfloat16)


def body(*arrays):
    seq_count, head_count = arrays[1].shape[:2]
    devices = lax.axis_size("seq")
    if seq_count == 1 and devices == head_count == EXPERTS == 16:
        return direct_body(*arrays)
    return split_body(*arrays)


def solution(mesh):
    in_specs = (
        P("groups", "seq", None),
        P("groups", None, "seq", None),
        P("groups", None, None),
        P("groups", "seq", None),
        P("groups", "seq", None),
        P("groups", "seq", None),
        P(None, "seq"),
        P("seq", None),
    )
    out_specs = P("groups", "seq", None)
    return jax.shard_map(body, mesh=mesh, in_specs=in_specs, out_specs=out_specs, check_vma=False)
```

```python
import functools
import math

import jax
import jax.numpy as jnp
from jax import lax
from jax.experimental import pallas as pl
from jax.experimental.pallas import tpu as pltpu
from jax.sharding import PartitionSpec as P

EXPERTS = 16
CAP = 8
FRAMES = 16
LAYER = 4
CODE_ROWS = 8
MIB = 2**20

VMEM = pl.BlockSpec(memory_space=pltpu.VMEM)
SMEM = pl.BlockSpec(memory_space=pltpu.SMEM)
HBM = pl.BlockSpec(memory_space=pltpu.HBM)


def held(array):
    return pltpu.with_memory_space_constraint(array, pltpu.VMEM)


def far(array):
    return pltpu.with_memory_space_constraint(array, pltpu.HBM)


def exchange(array):
    return lax.all_to_all(array, "seq", split_axis=0, concat_axis=0, tiled=True)


def slot_code(chosen, slot_assignment):
    return jnp.where(slot_assignment < CAP, chosen * CAP + slot_assignment, -1)


def one_hot(code, values=None, me=0):
    choices, count = code.shape
    row = lax.broadcasted_iota(jnp.int32, (EXPERTS * CAP, count), 0) ^ me * CAP
    hits = jnp.zeros(row.shape, jnp.float32)
    for i in range(choices):
        hits = hits + jnp.where(code[i : i + 1, :] == row, 1.0 if values is None else values[i : i + 1, :], 0.0)
    return hits


def frame_order(rows, transposed):
    each = rows // FRAMES
    out = lax.broadcasted_iota(jnp.int32, (rows, rows), 1 if transposed else 0)
    old = lax.broadcasted_iota(jnp.int32, (rows, rows), 0 if transposed else 1)
    return jnp.where(old == out % each * FRAMES + out // each, 1.0, 0.0).astype(jnp.bfloat16)


def prepare_kernel(
    me_ref, hidden_hbm, scales_hbm, ids_ref, slots_ref, gate_ref,
    scales_out, blending_out, *refs
):
    *outs, hidden, done = refs
    copies = [
        pltpu.make_async_copy(hidden_hbm, hidden, done.at[0]),
        pltpu.make_async_copy(scales_hbm, scales_out, done.at[1]),
    ]
    for copy in copies:
        copy.start()
    code = slot_code(ids_ref[...], slots_ref[...])
    count = code.shape[1]
    blending = one_hot(code, gate_ref[...]).T
    for i in range(3):
        part = blending.astype(jnp.bfloat16)
        blending_out[i * count : (i + 1) * count, :] = part
        blending = blending - part.astype(jnp.float32)
    chosen = one_hot(code, me=me_ref[0]).astype(jnp.bfloat16)
    for copy in copies:
        copy.wait()
    layers, packed, lanes = outs[0].shape
    rows = jnp.dot(chosen, hidden[...], preferred_element_type=jnp.float32)
    for h in range(0, packed // CAP, 2):
        pair = [
            rows[:, (h + i) * lanes : (h + i + 1) * lanes].reshape(layers, LAYER, CAP, lanes) for i in range(2)
        ]
        pair = jnp.concatenate(pair, axis=2).astype(jnp.bfloat16)
        part = slice(h * CAP, (h + 2) * CAP)
        for r, out in enumerate(outs):
            out[:, part, :] = pair[:, r]


def prepare(me, hidden, scales, ids, slots, gate, lanes):
    count, width = hidden.shape
    slot_count = EXPERTS * CAP
    layers = EXPERTS // LAYER
    block = (CAP * width // lanes, lanes)
    return pl.pallas_call(
        prepare_kernel,
        out_shape=[
            pltpu.VMEM(scales.shape, scales.dtype),
            pltpu.VMEM((3 * count, slot_count), jnp.bfloat16),
        ]
        + [jax.ShapeDtypeStruct((layers,) + block, hidden.dtype)] * LAYER,
        in_specs=[SMEM, HBM, HBM, VMEM, VMEM, VMEM],
        out_specs=[VMEM] * (2 + LAYER),
        scratch_shapes=[pltpu.VMEM(hidden.shape, hidden.dtype), pltpu.SemaphoreType.DMA((2,))],
        compiler_params=pltpu.CompilerParams(vmem_limit_bytes=16 * MIB),
        cost_estimate=pl.CostEstimate(flops=2 * slot_count * count * width, bytes_accessed=4 * MIB, transcendentals=0),
    )(me, far(hidden), far(scales), ids, slots, gate)


def by_layer_kernel(*refs):
    for r in range(LAYER):
        for i in range(1, LAYER):
            refs[LAYER + i - 1][r] = refs[r][i]


def by_layer(*blocks):
    return pl.pallas_call(
        by_layer_kernel,
        out_shape=[jax.ShapeDtypeStruct(blocks[0].shape, blocks[0].dtype)] * (LAYER - 1),
        in_specs=[VMEM] * LAYER,
        out_specs=[VMEM] * (LAYER - 1),
        compiler_params=pltpu.CompilerParams(vmem_limit_bytes=8 * MIB),
    )(*blocks)


def by_place_kernel(*refs):
    for i in range(LAYER):
        for r in range(LAYER):
            refs[LAYER + r][i] = refs[i][r]


def by_place(*blocks):
    return pl.pallas_call(
        by_place_kernel,
        out_shape=[jax.ShapeDtypeStruct(blocks[0].shape, blocks[0].dtype)] * LAYER,
        in_specs=[VMEM] * LAYER,
        out_specs=[VMEM] * LAYER,
        compiler_params=pltpu.CompilerParams(vmem_limit_bytes=8 * MIB),
    )(*blocks)


def assemble_kernel(me_ref, *refs):
    *block_refs, out_ref = refs
    here, away = block_refs[:LAYER], block_refs[LAYER:]
    for r in range(LAYER):
        for i in range(LAYER):
            out_ref[me_ref[0] ^ (LAYER * i + r)] = away[i - 1][r] if away and i else here[r][i]


def assemble(me, here, away=()):
    return pl.pallas_call(
        assemble_kernel,
        out_shape=jax.ShapeDtypeStruct((LAYER * LAYER,) + here[0].shape[1:], here[0].dtype),
        in_specs=[SMEM] + [VMEM] * (LAYER + len(away)),
        out_specs=VMEM,
        compiler_params=pltpu.CompilerParams(vmem_limit_bytes=8 * MIB),
    )(me, *here, *away)


def attention_kernel(me_ref, codes_ref, rows_ref, expert_out, attended_out, framed, attended, codes):
    sources, count, triple = rows_ref.shape
    width = triple // 3
    places = count // FRAMES
    piece = 2 * places
    order = frame_order(2 * count, False)
    for c in range(sources // 2):
        rows = rows_ref[2 * c : 2 * c + 2].reshape(2 * count, triple)
        rows = jnp.dot(order, rows, preferred_element_type=jnp.float32)
        framed[:, c * piece : (c + 1) * piece, :] = rows.astype(jnp.bfloat16).reshape(FRAMES, piece, triple)
    queries = framed[:, :, :width]
    keys = framed[:, :, width : 2 * width]
    values = framed[:, :, 2 * width :]
    scores = lax.dot_general(
        queries, keys, (((2,), (2,)), ((0,), (0,))), preferred_element_type=jnp.float32
    ) * width ** (-0.5)
    exponent = jnp.exp(scores - jnp.max(scores, axis=-1, keepdims=True))
    weights = (exponent / jnp.sum(exponent, axis=-1, keepdims=True)).astype(jnp.bfloat16)
    result = lax.dot_general(weights, values, (((2,), (1,)), ((0,), (0,))), preferred_element_type=jnp.float32)
    attended[...] = result.astype(jnp.bfloat16).astype(jnp.float32)
    codes[...] = jnp.zeros_like(codes)
    for s in range(sources):
        m = me_ref[0] ^ s
        codes[s * CODE_ROWS : s * CODE_ROWS + 2, :] = codes_ref[m // LAYER, m % LAYER].astype(jnp.float32)
    by_frame = lax.dot_general(
        codes[...].astype(jnp.bfloat16),
        frame_order(count, False),
        (((1,), (1,)), ((), ())),
        preferred_element_type=jnp.float32,
    )
    slot = lax.broadcasted_iota(jnp.int32, (EXPERTS * CAP, count), 0).astype(jnp.float32)
    for c in range(sources // 2):
        pair = []
        for s in (2 * c, 2 * c + 1):
            code = by_frame[s * CODE_ROWS : s * CODE_ROWS + 2]
            hit = (code[0:1] == slot) | (code[1:2] == slot)
            rows = attended[:, s * places : (s + 1) * places, :].reshape(count, width).astype(jnp.bfloat16)
            attended_out[s] = rows
            rows = jnp.dot(
                jnp.where(hit, 1.0, 0.0).astype(jnp.bfloat16), rows, preferred_element_type=jnp.float32
            )
            pair.append(rows.reshape(EXPERTS, CAP, width))
        expert_out[:, 2 * c * CAP : 2 * (c + 1) * CAP, :] = jnp.concatenate(pair, axis=1).astype(jnp.bfloat16)


def attention(me, codes, rows):
    sources, count, triple = rows.shape
    width = triple // 3
    by_frame = (FRAMES, sources * count // FRAMES)
    return pl.pallas_call(
        attention_kernel,
        out_shape=[
            jax.ShapeDtypeStruct((EXPERTS, sources * CAP, width), jnp.bfloat16),
            jax.ShapeDtypeStruct((sources, count, width), jnp.bfloat16),
        ],
        in_specs=[SMEM, VMEM, VMEM],
        out_specs=[VMEM] * 2,
        scratch_shapes=[
            pltpu.VMEM(by_frame + (triple,), jnp.bfloat16),
            pltpu.VMEM(by_frame + (width,), jnp.float32),
            pltpu.VMEM((sources * CODE_ROWS, count), jnp.float32),
        ],
        compiler_params=pltpu.CompilerParams(vmem_limit_bytes=24 * MIB),
    )(me, codes, rows)


def restore_kernel(me_ref, attended_ref, *outs):
    count = attended_ref.shape[1]
    back = frame_order(count, True)
    for m in range(LAYER * LAYER):
        rows = jnp.dot(back, attended_ref[me_ref[0] ^ m], preferred_element_type=jnp.float32)
        outs[m // LAYER][m % LAYER] = rows.astype(jnp.bfloat16)


def restore(me, attended):
    block = (LAYER,) + attended.shape[1:]
    return pl.pallas_call(
        restore_kernel,
        out_shape=[jax.ShapeDtypeStruct(block, attended.dtype)] * LAYER,
        in_specs=[SMEM, VMEM],
        out_specs=[VMEM] * LAYER,
        compiler_params=pltpu.CompilerParams(vmem_limit_bytes=16 * MIB),
        cost_estimate=pl.CostEstimate(flops=2**35, bytes_accessed=MIB, transcendentals=0),
    )(me, attended)


def normalize(resid, scales_ref):
    shifted = resid - jnp.mean(resid, axis=-1, keepdims=True)
    spread = jnp.mean(shifted * shifted, axis=-1, keepdims=True)
    normed = shifted * lax.rsqrt(spread + 1e-06) * (1.0 + scales_ref[2:3, :]) + scales_ref[1:2, :]
    return normed.astype(jnp.bfloat16)


def expert_kernel(
    block, arrived_ref, hidden_ref, scales_ref, first_hbm, second_hbm, out_ref,
    rows, total, first, second, first_done, second_done,
):
    blocks = first_hbm.shape[1] // block
    depth = first.shape[0]

    def fetch_first(step):
        place = lax.rem(step, depth)
        start = pl.multiple_of(step * block, block)
        return pltpu.make_async_copy(first_hbm.at[:, pl.ds(start, block)], first.at[place], first_done.at[place])

    def fetch_second(step):
        place = lax.rem(step, depth)
        start = pl.multiple_of(step * block, block)
        return pltpu.make_async_copy(second_hbm.at[pl.ds(start, block)], second.at[place], second_done.at[place])

    for step in range(min(depth, blocks)):
        fetch_first(step).start()
        fetch_second(step).start()
    total[...] = jnp.zeros_like(total)
    heads, count, lanes = arrived_ref.shape
    parts = []
    for h in range(heads):
        columns = slice(h * lanes, (h + 1) * lanes)
        hidden = hidden_ref[:, h * CAP : (h + 1) * CAP, :].astype(jnp.float32)
        mixed = arrived_ref[h].astype(jnp.float32)
        parts.append(hidden.reshape(count, lanes) + scales_ref[0:1, columns] * mixed)
    rows[...] = normalize(jnp.concatenate(parts, axis=1), scales_ref)

    def work(step, _):
        place = lax.rem(step, depth)
        fetch_first(step).wait()
        inner = jnp.dot(rows[...], first[place], preferred_element_type=jnp.float32)
        inner = jax.nn.gelu(inner, approximate=True).astype(jnp.bfloat16)

        @pl.when(step + depth < blocks)
        def _():
            fetch_first(step + depth).start()

        fetch_second(step).wait()
        total[...] += jnp.dot(inner, second[place], preferred_element_type=jnp.float32)

        @pl.when(step + depth < blocks)
        def _():
            fetch_second(step + depth).start()

        return 0

    lax.fori_loop(0, blocks, work, 0)
    out_ref[...] = total[...].astype(jnp.bfloat16)


def expert(arrived, hidden_rows, scales, first, second):
    width, hidden = first.shape
    count = arrived.shape[0] * CAP
    block = math.gcd(hidden, 1024)
    depth = min(hidden // block, 3)
    return pl.pallas_call(
        functools.partial(expert_kernel, block),
        out_shape=jax.ShapeDtypeStruct((count, width), jnp.bfloat16),
        in_specs=[VMEM] * 3 + [HBM, HBM],
        out_specs=VMEM,
        scratch_shapes=[
            pltpu.VMEM((count, width), jnp.bfloat16),
            pltpu.VMEM((count, width), jnp.float32),
            pltpu.VMEM((depth, width, block), jnp.bfloat16),
            pltpu.VMEM((depth, block, width), jnp.bfloat16),
            pltpu.SemaphoreType.DMA((depth,)),
            pltpu.SemaphoreType.DMA((depth,)),
        ],
        compiler_params=pltpu.CompilerParams(vmem_limit_bytes=44 * MIB),
        cost_estimate=pl.CostEstimate(
            flops=64 * count * width * hidden, bytes_accessed=4 * width * hidden, transcendentals=count * hidden
        ),
    )(arrived, hidden_rows, held(scales), far(first), far(second))


def residual_kernel(me_ref, *refs):
    *block_refs, hidden_ref, scales_ref, out_ref = refs
    lanes = block_refs[0].shape[2]
    for r in range(LAYER):
        for i in range(LAYER):
            head = me_ref[0] ^ (LAYER * i + r)
            columns = pl.ds(pl.multiple_of(head * lanes, lanes), lanes)
            mixed = block_refs[r][i].astype(jnp.float32)
            out_ref[:, columns] = hidden_ref[:, columns].astype(jnp.float32) + scales_ref[0:1, columns] * mixed


def residual(me, blocks, hidden, scales):
    return pl.pallas_call(
        residual_kernel,
        out_shape=pltpu.VMEM(hidden.shape, jnp.float32),
        in_specs=[SMEM] + [VMEM] * (LAYER + 2),
        out_specs=VMEM,
        compiler_params=pltpu.CompilerParams(vmem_limit_bytes=8 * MIB),
    )(me, *blocks, hidden, held(scales))


def combine_kernel(resid_ref, scales_ref, blending_ref, brought_ref, out_hbm, out, done):
    count, width = out.shape
    step = width // done.shape[0]
    copies = []
    for c in range(done.shape[0]):
        columns = slice(c * step, (c + 1) * step)
        mixture = jnp.dot(blending_ref[...], brought_ref[:, columns], preferred_element_type=jnp.float32)
        mixture = mixture[:count] + (mixture[count : 2 * count] + mixture[2 * count :])
        out[:, columns] = (resid_ref[:, columns] + scales_ref[3:4, columns] * mixture).astype(jnp.bfloat16)
        copies.append(pltpu.make_async_copy(out.at[:, columns], out_hbm.at[:, columns], done.at[c]))
        copies[-1].start()
    for copy in copies:
        copy.wait()


def combine(resid, scales, blending, brought):
    return pl.pallas_call(
        combine_kernel,
        out_shape=pltpu.HBM(resid.shape, jnp.bfloat16),
        in_specs=[VMEM] * 4,
        out_specs=HBM,
        scratch_shapes=[pltpu.VMEM(resid.shape, jnp.bfloat16), pltpu.SemaphoreType.DMA((4,))],
        compiler_params=pltpu.CompilerParams(vmem_limit_bytes=16 * MIB),
    )(held(resid), held(scales), held(blending), brought)


def partner(array, step):
    devices = lax.axis_size("seq")
    return lax.ppermute(array, "seq", [(i, i ^ step) for i in range(devices)])


def within_layer(stay, *blocks):
    return [stay] + [partner(block, r + 1) for r, block in enumerate(blocks)]


def across_layers(stay, *blocks):
    return [stay] + [partner(block, LAYER * (i + 1)) for i, block in enumerate(blocks)]


def gather_codes(code):
    layer = jnp.stack(within_layer(*[code] * LAYER))
    return jnp.stack(across_layers(*[layer] * LAYER))


def direct_body(hidden_in, qkv, modulation, route_weight, expert_ids, slots, w_in, w_out):
    triple = qkv.shape[3]
    devices = lax.axis_size("seq")
    me = jnp.full((1,), lax.axis_index("seq"), jnp.int32)
    ids, slot_rows = expert_ids[0].T, slots[0].T
    owned = exchange(qkv[0])
    codes = gather_codes(slot_code(ids, slot_rows))
    scales, blending, *here = prepare(
        me, hidden_in[0], modulation[0], ids, slot_rows, route_weight[0].T, triple // 3
    )
    here = within_layer(*here)
    near, *away = by_layer(*here)
    near, *away, owned = lax.optimization_barrier((partner(near, LAYER), *away, owned))
    away = [near, partner(away[0], 2 * LAYER), partner(away[1], 3 * LAYER)]
    to_experts, attended = attention(me, codes, owned)
    arrived = exchange(to_experts)
    hidden_rows, attended = lax.optimization_barrier((assemble(me, here, away), attended))
    stay, *away = restore(me, attended)
    *away, arrived = lax.optimization_barrier((*away, arrived))
    away = across_layers(stay, *away)
    computed = expert(arrived, hidden_rows, scales, w_in, w_out)
    *away, computed = lax.optimization_barrier((*away, computed))
    brought = exchange(computed.reshape(devices, CAP, -1))
    resid = residual(me, within_layer(*by_place(*away)), hidden_in[0], scales)
    return combine(resid, scales, blending, brought.reshape(devices * CAP, -1))[None]


def attend(queries, key_rows, values):
    length, width = queries.shape
    block_rows = math.gcd(length, 512)
    stacked = queries.reshape(length // block_rows, block_rows, width)

    def scores_for(query_block):
        scores = jnp.dot(query_block, key_rows.T, preferred_element_type=jnp.float32) * width ** (-0.5)
        scores = scores - jnp.max(scores, axis=-1, keepdims=True)
        exponent = jnp.exp(scores)
        weights = (exponent / jnp.sum(exponent, axis=-1, keepdims=True)).astype(jnp.bfloat16)
        return jnp.dot(weights, values, preferred_element_type=jnp.float32).astype(jnp.bfloat16)

    return lax.map(scores_for, stacked).reshape(length, width)


def split_body(hidden_in, qkv, modulation, route_weight, expert_ids, slots, w_in, w_out):
    seq_count, head_count, row_count, triple = qkv.shape
    head_width = triple // 3
    width = head_count * head_width
    devices_seq = lax.axis_size("seq")
    frame_parts = devices_seq // (seq_count * head_count)
    local_frames = FRAMES // frame_parts
    places = row_count // FRAMES
    arranged = qkv.reshape(seq_count, head_count, places, frame_parts, local_frames, triple)
    arranged = arranged.transpose(0, 1, 3, 2, 4, 5).reshape(devices_seq, places, local_frames, triple)
    owned = lax.all_to_all(arranged, "seq", split_axis=0, concat_axis=1, tiled=True)[0]
    by_frame = owned.transpose(1, 0, 2)
    attended = lax.map(
        lambda one_frame: attend(
            one_frame[:, :head_width],
            one_frame[:, head_width : 2 * head_width],
            one_frame[:, 2 * head_width :],
        ),
        by_frame,
    )
    outgoing = attended.transpose(1, 0, 2).reshape(devices_seq, places, local_frames, head_width)
    returned = exchange(outgoing)
    mixed = returned.reshape(seq_count, head_count, frame_parts, places, local_frames, head_width)
    mixed = mixed.transpose(0, 3, 2, 4, 1, 5).reshape(seq_count, row_count, width)
    resid = hidden_in.astype(jnp.float32) + modulation[:, 0][:, None, :] * mixed.astype(jnp.float32)
    center = jnp.mean(resid, axis=-1, keepdims=True)
    shifted = resid - center
    spread = jnp.mean(shifted * shifted, axis=-1, keepdims=True)
    normed = shifted * lax.rsqrt(spread + 1e-06)
    normed = (normed * (1.0 + modulation[:, 2][:, None, :]) + modulation[:, 1][:, None, :]).astype(jnp.bfloat16)
    token_rows = normed.reshape(seq_count * row_count, width)
    choice_count = expert_ids.shape[-1]
    code = slot_code(expert_ids, slots).reshape(-1, choice_count)
    weight = route_weight.reshape(-1, choice_count)
    hits = code[:, :, None] == jnp.arange(EXPERTS * CAP, dtype=jnp.int32)
    selected_expert = jnp.sum(hits, axis=1).astype(jnp.bfloat16)
    expert_blending = jnp.sum(jnp.where(hits, weight[:, :, None], 0.0), axis=1)
    gathered = jnp.einsum(
        "tk,td->kd", selected_expert, token_rows, preferred_element_type=jnp.float32
    ).astype(jnp.bfloat16)
    shards = devices_seq // EXPERTS
    spread_rows = jnp.broadcast_to(
        gathered.reshape(EXPERTS, 1, CAP, width), (EXPERTS, shards, CAP, width)
    ).reshape(devices_seq, CAP, width)
    arrived = exchange(spread_rows)
    inner = jax.nn.gelu(
        jnp.dot(arrived.reshape(-1, width), w_in, preferred_element_type=jnp.float32), approximate=True
    ).astype(jnp.bfloat16)
    computed = jnp.dot(inner, w_out, preferred_element_type=jnp.float32).astype(jnp.bfloat16)
    brought = exchange(computed.reshape(arrived.shape))
    combined_outputs = jnp.sum(
        brought.astype(jnp.float32).reshape(EXPERTS, shards, CAP, width), axis=1
    ).reshape(EXPERTS * CAP, width)
    mixture = jnp.dot(
        expert_blending, combined_outputs, precision=lax.Precision.HIGHEST, preferred_element_type=jnp.float32
    )
    final = resid + modulation[:, 3][:, None, :] * mixture.reshape(seq_count, row_count, width)
    return final.astype(jnp.bfloat16)


def body(*arrays):
    seq_count, head_count = arrays[1].shape[:2]
    devices = lax.axis_size("seq")
    if seq_count == 1 and devices == head_count == EXPERTS == 16:
        return direct_body(*arrays)
    return split_body(*arrays)


def solution(mesh):
    in_specs = (
        P("groups", "seq", None),
        P("groups", None, "seq", None),
        P("groups", None, None),
        P("groups", "seq", None),
        P("groups", "seq", None),
        P("groups", "seq", None),
        P(None, "seq"),
        P("seq", None),
    )
    out_specs = P("groups", "seq", None)
    return jax.shard_map(body, mesh=mesh, in_specs=in_specs, out_specs=out_specs, check_vma=False)
```

```python
import functools
import math

import jax
import jax.numpy as jnp
from jax import lax
from jax.experimental import pallas as pl
from jax.experimental.pallas import tpu as pltpu
from jax.sharding import PartitionSpec as P

EXPERTS = 16
CAP = 8
FRAMES = 16
LAYER = 4
CODE_ROWS = 8
MIB = 2**20

VMEM = pl.BlockSpec(memory_space=pltpu.VMEM)
SMEM = pl.BlockSpec(memory_space=pltpu.SMEM)
HBM = pl.BlockSpec(memory_space=pltpu.HBM)


def held(array):
    return pltpu.with_memory_space_constraint(array, pltpu.VMEM)


def far(array):
    return pltpu.with_memory_space_constraint(array, pltpu.HBM)


def exchange(array):
    return lax.all_to_all(array, "seq", split_axis=0, concat_axis=0, tiled=True)


def slot_code(chosen, slot_assignment):
    return jnp.where(slot_assignment < CAP, chosen * CAP + slot_assignment, -1)


def one_hot(code, values=None, me=0):
    choices, count = code.shape
    row = lax.broadcasted_iota(jnp.int32, (EXPERTS * CAP, count), 0) ^ me * CAP
    hits = jnp.zeros(row.shape, jnp.float32)
    for i in range(choices):
        hits = hits + jnp.where(code[i : i + 1, :] == row, 1.0 if values is None else values[i : i + 1, :], 0.0)
    return hits


def frame_order(rows, transposed):
    each = rows // FRAMES
    out = lax.broadcasted_iota(jnp.int32, (rows, rows), 1 if transposed else 0)
    old = lax.broadcasted_iota(jnp.int32, (rows, rows), 0 if transposed else 1)
    return jnp.where(old == out % each * FRAMES + out // each, 1.0, 0.0).astype(jnp.bfloat16)


def prepare_kernel(
    me_ref, hidden_hbm, scales_hbm, ids_ref, slots_ref, gate_ref,
    scales_out, blending_out, *refs
):
    *outs, hidden, done = refs
    copies = [
        pltpu.make_async_copy(hidden_hbm, hidden, done.at[0]),
        pltpu.make_async_copy(scales_hbm, scales_out, done.at[1]),
    ]
    for copy in copies:
        copy.start()
    code = slot_code(ids_ref[...], slots_ref[...])
    count = code.shape[1]
    blending = one_hot(code, gate_ref[...]).T
    for i in range(3):
        part = blending.astype(jnp.bfloat16)
        blending_out[i * count : (i + 1) * count, :] = part
        blending = blending - part.astype(jnp.float32)
    chosen = one_hot(code, me=me_ref[0]).astype(jnp.bfloat16)
    for copy in copies:
        copy.wait()
    layers, packed, lanes = outs[0].shape
    rows = jnp.dot(chosen, hidden[...], preferred_element_type=jnp.float32)
    for h in range(0, packed // CAP, 2):
        pair = [
            rows[:, (h + i) * lanes : (h + i + 1) * lanes].reshape(layers, LAYER, CAP, lanes) for i in range(2)
        ]
        pair = jnp.concatenate(pair, axis=2).astype(jnp.bfloat16)
        part = slice(h * CAP, (h + 2) * CAP)
        for r, out in enumerate(outs):
            out[:, part, :] = pair[:, r]


def prepare(me, hidden, scales, ids, slots, gate, lanes):
    count, width = hidden.shape
    slot_count = EXPERTS * CAP
    layers = EXPERTS // LAYER
    block = (CAP * width // lanes, lanes)
    return pl.pallas_call(
        prepare_kernel,
        out_shape=[
            pltpu.VMEM(scales.shape, scales.dtype),
            pltpu.VMEM((3 * count, slot_count), jnp.bfloat16),
        ]
        + [jax.ShapeDtypeStruct((layers,) + block, hidden.dtype)] * LAYER,
        in_specs=[SMEM, HBM, HBM, VMEM, VMEM, VMEM],
        out_specs=[VMEM] * (2 + LAYER),
        scratch_shapes=[pltpu.VMEM(hidden.shape, hidden.dtype), pltpu.SemaphoreType.DMA((2,))],
        compiler_params=pltpu.CompilerParams(vmem_limit_bytes=16 * MIB),
        cost_estimate=pl.CostEstimate(flops=2 * slot_count * count * width, bytes_accessed=4 * MIB, transcendentals=0),
    )(me, far(hidden), far(scales), ids, slots, gate)


def by_layer_kernel(*refs):
    for r in range(LAYER):
        for i in range(1, LAYER):
            refs[LAYER + i - 1][r] = refs[r][i]


def by_layer(*blocks):
    return pl.pallas_call(
        by_layer_kernel,
        out_shape=[jax.ShapeDtypeStruct(blocks[0].shape, blocks[0].dtype)] * (LAYER - 1),
        in_specs=[VMEM] * LAYER,
        out_specs=[VMEM] * (LAYER - 1),
        compiler_params=pltpu.CompilerParams(vmem_limit_bytes=8 * MIB),
    )(*blocks)


def by_place_kernel(*refs):
    for i in range(LAYER):
        for r in range(LAYER):
            refs[LAYER + r][i] = refs[i][r]


def by_place(*blocks):
    return pl.pallas_call(
        by_place_kernel,
        out_shape=[jax.ShapeDtypeStruct(blocks[0].shape, blocks[0].dtype)] * LAYER,
        in_specs=[VMEM] * LAYER,
        out_specs=[VMEM] * LAYER,
        compiler_params=pltpu.CompilerParams(vmem_limit_bytes=8 * MIB),
    )(*blocks)


def assemble_kernel(me_ref, *refs):
    *block_refs, out_ref = refs
    here, away = block_refs[:LAYER], block_refs[LAYER:]
    for r in range(LAYER):
        for i in range(LAYER):
            out_ref[me_ref[0] ^ (LAYER * i + r)] = away[i - 1][r] if away and i else here[r][i]


def assemble(me, here, away=()):
    return pl.pallas_call(
        assemble_kernel,
        out_shape=jax.ShapeDtypeStruct((LAYER * LAYER,) + here[0].shape[1:], here[0].dtype),
        in_specs=[SMEM] + [VMEM] * (LAYER + len(away)),
        out_specs=VMEM,
        compiler_params=pltpu.CompilerParams(vmem_limit_bytes=8 * MIB),
    )(me, *here, *away)


def attention_kernel(me_ref, codes_ref, rows_ref, *refs):
    *outs, framed, attended, codes = refs
    slot_outs, place_outs = outs[:LAYER], outs[LAYER:]
    sources, count, triple = rows_ref.shape
    width = triple // 3
    places = count // FRAMES
    piece = 2 * places
    order = frame_order(2 * count, False)
    for c in range(sources // 2):
        rows = rows_ref[2 * c : 2 * c + 2].reshape(2 * count, triple)
        rows = jnp.dot(order, rows, preferred_element_type=jnp.float32)
        framed[:, c * piece : (c + 1) * piece, :] = rows.astype(jnp.bfloat16).reshape(FRAMES, piece, triple)
    queries = framed[:, :, :width]
    keys = framed[:, :, width : 2 * width]
    values = framed[:, :, 2 * width :]
    scores = lax.dot_general(
        queries, keys, (((2,), (2,)), ((0,), (0,))), preferred_element_type=jnp.float32
    ) * width ** (-0.5)
    exponent = jnp.exp(scores - jnp.max(scores, axis=-1, keepdims=True))
    weights = (exponent / jnp.sum(exponent, axis=-1, keepdims=True)).astype(jnp.bfloat16)
    result = lax.dot_general(weights, values, (((2,), (1,)), ((0,), (0,))), preferred_element_type=jnp.float32)
    attended[...] = result.astype(jnp.bfloat16).astype(jnp.float32)
    codes[...] = jnp.zeros_like(codes)
    for s in range(sources):
        m = me_ref[0] ^ s
        codes[s * CODE_ROWS : s * CODE_ROWS + 2, :] = codes_ref[m // LAYER, m % LAYER].astype(jnp.float32)
    by_frame = lax.dot_general(
        codes[...].astype(jnp.bfloat16),
        frame_order(count, False),
        (((1,), (1,)), ((), ())),
        preferred_element_type=jnp.float32,
    )
    slot = lax.broadcasted_iota(jnp.int32, (EXPERTS * CAP, count), 0) ^ me_ref[0] * CAP
    slot = slot.astype(jnp.float32)
    for c in range(sources // 2):
        pair = []
        for s in (2 * c, 2 * c + 1):
            code = by_frame[s * CODE_ROWS : s * CODE_ROWS + 2]
            hit = (code[0:1] == slot) | (code[1:2] == slot)
            rows = attended[:, s * places : (s + 1) * places, :].reshape(count, width).astype(jnp.bfloat16)
            rows = jnp.dot(
                jnp.where(hit, 1.0, 0.0).astype(jnp.bfloat16), rows, preferred_element_type=jnp.float32
            )
            pair.append(rows.reshape(EXPERTS // LAYER, LAYER, CAP, width))
        pair = jnp.concatenate(pair, axis=2).astype(jnp.bfloat16)
        for r, out in enumerate(slot_outs):
            out[:, 2 * c * CAP : 2 * (c + 1) * CAP, :] = pair[:, r]
    back = frame_order(count, True)
    for i, out in enumerate(place_outs):
        for r in range(LAYER):
            start = pl.multiple_of((me_ref[0] ^ (LAYER * i + r)) * places, places)
            rows = attended[:, pl.ds(start, places), :].reshape(count, width).astype(jnp.bfloat16)
            out[r] = jnp.dot(back, rows, preferred_element_type=jnp.float32).astype(jnp.bfloat16)


def attention(me, codes, rows):
    sources, count, triple = rows.shape
    width = triple // 3
    by_frame = (FRAMES, sources * count // FRAMES)
    shapes = [(EXPERTS // LAYER, sources * CAP, width)] * LAYER + [(sources // LAYER, count, width)] * LAYER
    outs = pl.pallas_call(
        attention_kernel,
        out_shape=[jax.ShapeDtypeStruct(shape, jnp.bfloat16) for shape in shapes],
        in_specs=[SMEM, VMEM, VMEM],
        out_specs=[VMEM] * len(shapes),
        scratch_shapes=[
            pltpu.VMEM(by_frame + (triple,), jnp.bfloat16),
            pltpu.VMEM(by_frame + (width,), jnp.float32),
            pltpu.VMEM((sources * CODE_ROWS, count), jnp.float32),
        ],
        compiler_params=pltpu.CompilerParams(vmem_limit_bytes=20 * MIB),
        cost_estimate=pl.CostEstimate(flops=2**36, bytes_accessed=4 * MIB, transcendentals=0),
    )(me, codes, rows)
    return outs[:LAYER], outs[LAYER:]


def normalize(resid, scales_ref):
    shifted = resid - jnp.mean(resid, axis=-1, keepdims=True)
    spread = jnp.mean(shifted * shifted, axis=-1, keepdims=True)
    normed = shifted * lax.rsqrt(spread + 1e-06) * (1.0 + scales_ref[2:3, :]) + scales_ref[1:2, :]
    return normed.astype(jnp.bfloat16)


def stage_kernel(first_hbm, after_ref, first_out, done):
    del after_ref
    copy = pltpu.make_async_copy(first_hbm.at[:, pl.ds(0, first_out.shape[1])], first_out, done)
    copy.start()
    copy.wait()


def stage(first, columns, after):
    return pl.pallas_call(
        stage_kernel,
        out_shape=pltpu.VMEM((first.shape[0], columns), first.dtype),
        in_specs=[HBM, VMEM],
        out_specs=VMEM,
        scratch_shapes=[pltpu.SemaphoreType.DMA],
        compiler_params=pltpu.CompilerParams(vmem_limit_bytes=4 * MIB),
        cost_estimate=pl.CostEstimate(flops=0, bytes_accessed=4 * first.shape[0] * columns, transcendentals=0),
    )(far(first), after)


def expert_kernel(block, arrived_ref, hidden_ref, scales_ref, first_ref, second_hbm, out_ref, rows, total, ring, done):
    blocks = first_ref.shape[1] // block
    depth = ring.shape[0]

    def fetch(step):
        place = lax.rem(step, depth)
        part = pl.ds(pl.multiple_of(step * block, block), block)
        return pltpu.make_async_copy(second_hbm.at[part], ring.at[place], done.at[place])

    for step in range(min(depth, blocks)):
        fetch(step).start()
    total[...] = jnp.zeros_like(total)
    heads, count, lanes = arrived_ref.shape
    parts = []
    for h in range(heads):
        columns = slice(h * lanes, (h + 1) * lanes)
        hidden = hidden_ref[:, h * CAP : (h + 1) * CAP, :].astype(jnp.float32)
        mixed = arrived_ref[h].astype(jnp.float32)
        parts.append(hidden.reshape(count, lanes) + scales_ref[0:1, columns] * mixed)
    rows[...] = normalize(jnp.concatenate(parts, axis=1), scales_ref)

    def work(step, _):
        columns = pl.ds(pl.multiple_of(step * block, block), block)
        inner = jnp.dot(rows[...], first_ref[:, columns], preferred_element_type=jnp.float32)
        inner = jax.nn.gelu(inner, approximate=True).astype(jnp.bfloat16)
        fetch(step).wait()
        total[...] += jnp.dot(inner, ring[lax.rem(step, depth)], preferred_element_type=jnp.float32)

        @pl.when(step + depth < blocks)
        def _():
            fetch(step + depth).start()

        return 0

    lax.fori_loop(0, blocks, work, 0)
    out_ref[...] = total[...].astype(jnp.bfloat16)


def expert(arrived, hidden_rows, scales, first, second):
    width, hidden = first.shape
    count = arrived.shape[0] * CAP
    block = math.gcd(hidden, 1024)
    depth = min(hidden // block, 3)
    return pl.pallas_call(
        functools.partial(expert_kernel, block),
        out_shape=jax.ShapeDtypeStruct((count, width), jnp.bfloat16),
        in_specs=[VMEM] * 4 + [HBM],
        out_specs=VMEM,
        scratch_shapes=[
            pltpu.VMEM((count, width), jnp.bfloat16),
            pltpu.VMEM((count, width), jnp.float32),
            pltpu.VMEM((depth, block, width), jnp.bfloat16),
            pltpu.SemaphoreType.DMA((depth,)),
        ],
        compiler_params=pltpu.CompilerParams(vmem_limit_bytes=22 * MIB),
        cost_estimate=pl.CostEstimate(
            flops=64 * count * width * hidden, bytes_accessed=2 * width * hidden, transcendentals=count * hidden
        ),
    )(held(arrived), held(hidden_rows), held(scales), held(first), far(second))


def residual_kernel(me_ref, *refs):
    *block_refs, hidden_ref, scales_ref, out_ref = refs
    lanes = block_refs[0].shape[2]
    for r in range(LAYER):
        for i in range(LAYER):
            head = me_ref[0] ^ (LAYER * i + r)
            columns = pl.ds(pl.multiple_of(head * lanes, lanes), lanes)
            mixed = block_refs[r][i].astype(jnp.float32)
            out_ref[:, columns] = hidden_ref[:, columns].astype(jnp.float32) + scales_ref[0:1, columns] * mixed


def residual(me, blocks, hidden, scales):
    return pl.pallas_call(
        residual_kernel,
        out_shape=pltpu.VMEM(hidden.shape, jnp.float32),
        in_specs=[SMEM] + [VMEM] * (LAYER + 2),
        out_specs=VMEM,
        compiler_params=pltpu.CompilerParams(vmem_limit_bytes=8 * MIB),
    )(me, *blocks, hidden, held(scales))


def combine_kernel(resid_ref, scales_ref, blending_ref, brought_ref, out_hbm, out, done):
    count, width = out.shape
    step = width // done.shape[0]
    copies = []
    for c in range(done.shape[0]):
        columns = slice(c * step, (c + 1) * step)
        mixture = jnp.dot(blending_ref[...], brought_ref[:, columns], preferred_element_type=jnp.float32)
        mixture = mixture[:count] + (mixture[count : 2 * count] + mixture[2 * count :])
        out[:, columns] = (resid_ref[:, columns] + scales_ref[3:4, columns] * mixture).astype(jnp.bfloat16)
        copies.append(pltpu.make_async_copy(out.at[:, columns], out_hbm.at[:, columns], done.at[c]))
        copies[-1].start()
    for copy in copies:
        copy.wait()


def combine(resid, scales, blending, brought):
    return pl.pallas_call(
        combine_kernel,
        out_shape=pltpu.HBM(resid.shape, jnp.bfloat16),
        in_specs=[VMEM] * 4,
        out_specs=HBM,
        scratch_shapes=[pltpu.VMEM(resid.shape, jnp.bfloat16), pltpu.SemaphoreType.DMA((4,))],
        compiler_params=pltpu.CompilerParams(vmem_limit_bytes=16 * MIB),
    )(held(resid), held(scales), held(blending), brought)


def partner(array, step):
    devices = lax.axis_size("seq")
    return lax.ppermute(array, "seq", [(i, i ^ step) for i in range(devices)])


def within_layer(stay, *blocks):
    return [stay] + [partner(block, r + 1) for r, block in enumerate(blocks)]


def across_layers(*blocks):
    return [partner(block, LAYER * (i + 1)) for i, block in enumerate(blocks)]


def gather_codes(code):
    layer = jnp.stack(within_layer(*[code] * LAYER))
    return jnp.stack([layer] + across_layers(*[layer] * (LAYER - 1)))


def direct_body(hidden_in, qkv, modulation, route_weight, expert_ids, slots, w_in, w_out):
    triple = qkv.shape[3]
    devices = lax.axis_size("seq")
    me = jnp.full((1,), lax.axis_index("seq"), jnp.int32)
    ids, slot_rows = expert_ids[0].T, slots[0].T
    owned = exchange(qkv[0])
    codes = gather_codes(slot_code(ids, slot_rows))
    scales, blending, *here = prepare(
        me, hidden_in[0], modulation[0], ids, slot_rows, route_weight[0].T, triple // 3
    )
    here = within_layer(*here)
    near, *away = by_layer(*here)
    near, *away, owned = lax.optimization_barrier((partner(near, LAYER), *away, owned))
    away = [near, partner(away[0], 2 * LAYER), partner(away[1], 3 * LAYER)]
    slot_blocks, (stay, *places) = attention(me, codes, owned)
    slots_here = within_layer(*slot_blocks)
    slots_away = by_layer(*slots_here)
    staged = stage(w_in, w_in.shape[1], slots_away[0])
    slots_away = across_layers(*slots_away)
    hidden_rows = assemble(me, here, away)
    arrived = assemble(me, slots_here, slots_away)
    *places, arrived = lax.optimization_barrier((*places, arrived))
    places = across_layers(*places)
    computed = expert(arrived, hidden_rows, scales, staged, w_out)
    *places, computed = lax.optimization_barrier((*places, computed))
    brought = exchange(computed.reshape(devices, CAP, -1))
    resid = residual(me, within_layer(*by_place(stay, *places)), hidden_in[0], scales)
    return combine(resid, scales, blending, brought.reshape(devices * CAP, -1))[None]


def attend(queries, key_rows, values):
    length, width = queries.shape
    block_rows = math.gcd(length, 512)
    stacked = queries.reshape(length // block_rows, block_rows, width)

    def scores_for(query_block):
        scores = jnp.dot(query_block, key_rows.T, preferred_element_type=jnp.float32) * width ** (-0.5)
        scores = scores - jnp.max(scores, axis=-1, keepdims=True)
        exponent = jnp.exp(scores)
        weights = (exponent / jnp.sum(exponent, axis=-1, keepdims=True)).astype(jnp.bfloat16)
        return jnp.dot(weights, values, preferred_element_type=jnp.float32).astype(jnp.bfloat16)

    return lax.map(scores_for, stacked).reshape(length, width)


def split_body(hidden_in, qkv, modulation, route_weight, expert_ids, slots, w_in, w_out):
    seq_count, head_count, row_count, triple = qkv.shape
    head_width = triple // 3
    width = head_count * head_width
    devices_seq = lax.axis_size("seq")
    frame_parts = devices_seq // (seq_count * head_count)
    local_frames = FRAMES // frame_parts
    places = row_count // FRAMES
    arranged = qkv.reshape(seq_count, head_count, places, frame_parts, local_frames, triple)
    arranged = arranged.transpose(0, 1, 3, 2, 4, 5).reshape(devices_seq, places, local_frames, triple)
    owned = lax.all_to_all(arranged, "seq", split_axis=0, concat_axis=1, tiled=True)[0]
    by_frame = owned.transpose(1, 0, 2)
    attended = lax.map(
        lambda one_frame: attend(
            one_frame[:, :head_width],
            one_frame[:, head_width : 2 * head_width],
            one_frame[:, 2 * head_width :],
        ),
        by_frame,
    )
    outgoing = attended.transpose(1, 0, 2).reshape(devices_seq, places, local_frames, head_width)
    returned = exchange(outgoing)
    mixed = returned.reshape(seq_count, head_count, frame_parts, places, local_frames, head_width)
    mixed = mixed.transpose(0, 3, 2, 4, 1, 5).reshape(seq_count, row_count, width)
    resid = hidden_in.astype(jnp.float32) + modulation[:, 0][:, None, :] * mixed.astype(jnp.float32)
    center = jnp.mean(resid, axis=-1, keepdims=True)
    shifted = resid - center
    spread = jnp.mean(shifted * shifted, axis=-1, keepdims=True)
    normed = shifted * lax.rsqrt(spread + 1e-06)
    normed = (normed * (1.0 + modulation[:, 2][:, None, :]) + modulation[:, 1][:, None, :]).astype(jnp.bfloat16)
    token_rows = normed.reshape(seq_count * row_count, width)
    choice_count = expert_ids.shape[-1]
    code = slot_code(expert_ids, slots).reshape(-1, choice_count)
    weight = route_weight.reshape(-1, choice_count)
    hits = code[:, :, None] == jnp.arange(EXPERTS * CAP, dtype=jnp.int32)
    selected_expert = jnp.sum(hits, axis=1).astype(jnp.bfloat16)
    expert_blending = jnp.sum(jnp.where(hits, weight[:, :, None], 0.0), axis=1)
    gathered = jnp.einsum(
        "tk,td->kd", selected_expert, token_rows, preferred_element_type=jnp.float32
    ).astype(jnp.bfloat16)
    shards = devices_seq // EXPERTS
    spread_rows = jnp.broadcast_to(
        gathered.reshape(EXPERTS, 1, CAP, width), (EXPERTS, shards, CAP, width)
    ).reshape(devices_seq, CAP, width)
    arrived = exchange(spread_rows)
    inner = jax.nn.gelu(
        jnp.dot(arrived.reshape(-1, width), w_in, preferred_element_type=jnp.float32), approximate=True
    ).astype(jnp.bfloat16)
    computed = jnp.dot(inner, w_out, preferred_element_type=jnp.float32).astype(jnp.bfloat16)
    brought = exchange(computed.reshape(arrived.shape))
    combined_outputs = jnp.sum(
        brought.astype(jnp.float32).reshape(EXPERTS, shards, CAP, width), axis=1
    ).reshape(EXPERTS * CAP, width)
    mixture = jnp.dot(
        expert_blending, combined_outputs, precision=lax.Precision.HIGHEST, preferred_element_type=jnp.float32
    )
    final = resid + modulation[:, 3][:, None, :] * mixture.reshape(seq_count, row_count, width)
    return final.astype(jnp.bfloat16)


def body(*arrays):
    seq_count, head_count = arrays[1].shape[:2]
    devices = lax.axis_size("seq")
    if seq_count == 1 and devices == head_count == EXPERTS == 16:
        return direct_body(*arrays)
    return split_body(*arrays)


def solution(mesh):
    in_specs = (
        P("groups", "seq", None),
        P("groups", None, "seq", None),
        P("groups", None, None),
        P("groups", "seq", None),
        P("groups", "seq", None),
        P("groups", "seq", None),
        P(None, "seq"),
        P("seq", None),
    )
    out_specs = P("groups", "seq", None)
    return jax.shard_map(body, mesh=mesh, in_specs=in_specs, out_specs=out_specs, check_vma=False)
```

```python
import functools
import math

import jax
import jax.numpy as jnp
from jax import lax
from jax.experimental import pallas as pl
from jax.experimental.pallas import tpu as pltpu
from jax.sharding import PartitionSpec as P

EXPERTS = 16
CAP = 8
FRAMES = 16
LAYER = 4
CODE_ROWS = 8
MIB = 2**20

VMEM = pl.BlockSpec(memory_space=pltpu.VMEM)
SMEM = pl.BlockSpec(memory_space=pltpu.SMEM)
HBM = pl.BlockSpec(memory_space=pltpu.HBM)


def held(array):
    return pltpu.with_memory_space_constraint(array, pltpu.VMEM)


def far(array):
    return pltpu.with_memory_space_constraint(array, pltpu.HBM)


def exchange(array):
    return lax.all_to_all(array, "seq", split_axis=0, concat_axis=0, tiled=True)


def slot_code(chosen, slot_assignment):
    return jnp.where(slot_assignment < CAP, chosen * CAP + slot_assignment, -1)


def one_hot(code, values=None, me=0):
    choices, count = code.shape
    row = lax.broadcasted_iota(jnp.int32, (EXPERTS * CAP, count), 0) ^ me * CAP
    hits = jnp.zeros(row.shape, jnp.float32)
    for i in range(choices):
        hits = hits + jnp.where(code[i : i + 1, :] == row, 1.0 if values is None else values[i : i + 1, :], 0.0)
    return hits


def frame_order(rows, transposed):
    each = rows // FRAMES
    out = lax.broadcasted_iota(jnp.int32, (rows, rows), 1 if transposed else 0)
    old = lax.broadcasted_iota(jnp.int32, (rows, rows), 0 if transposed else 1)
    return jnp.where(old == out % each * FRAMES + out // each, 1.0, 0.0).astype(jnp.bfloat16)


def prepare_kernel(
    me_ref, hidden_hbm, scales_hbm, ids_ref, slots_ref, gate_ref,
    scales_out, blending_out, *refs
):
    *outs, hidden, done = refs
    copies = [
        pltpu.make_async_copy(hidden_hbm, hidden, done.at[0]),
        pltpu.make_async_copy(scales_hbm, scales_out, done.at[1]),
    ]
    for copy in copies:
        copy.start()
    code = slot_code(ids_ref[...], slots_ref[...])
    count = code.shape[1]
    blending = one_hot(code, gate_ref[...]).T
    for i in range(3):
        part = blending.astype(jnp.bfloat16)
        blending_out[i * count : (i + 1) * count, :] = part
        blending = blending - part.astype(jnp.float32)
    chosen = one_hot(code, me=me_ref[0]).astype(jnp.bfloat16)
    for copy in copies:
        copy.wait()
    layers, packed, lanes = outs[0].shape
    rows = jnp.dot(chosen, hidden[...], preferred_element_type=jnp.float32)
    for h in range(0, packed // CAP, 2):
        pair = [
            rows[:, (h + i) * lanes : (h + i + 1) * lanes].reshape(layers, LAYER, CAP, lanes) for i in range(2)
        ]
        pair = jnp.concatenate(pair, axis=2).astype(jnp.bfloat16)
        part = slice(h * CAP, (h + 2) * CAP)
        for r, out in enumerate(outs):
            out[:, part, :] = pair[:, r]


def prepare(me, hidden, scales, ids, slots, gate, lanes):
    count, width = hidden.shape
    slot_count = EXPERTS * CAP
    layers = EXPERTS // LAYER
    block = (CAP * width // lanes, lanes)
    return pl.pallas_call(
        prepare_kernel,
        out_shape=[
            pltpu.VMEM(scales.shape, scales.dtype),
            pltpu.VMEM((3 * count, slot_count), jnp.bfloat16),
        ]
        + [jax.ShapeDtypeStruct((layers,) + block, hidden.dtype)] * LAYER,
        in_specs=[SMEM, HBM, HBM, VMEM, VMEM, VMEM],
        out_specs=[VMEM] * (2 + LAYER),
        scratch_shapes=[pltpu.VMEM(hidden.shape, hidden.dtype), pltpu.SemaphoreType.DMA((2,))],
        compiler_params=pltpu.CompilerParams(vmem_limit_bytes=16 * MIB),
        cost_estimate=pl.CostEstimate(flops=2 * slot_count * count * width, bytes_accessed=4 * MIB, transcendentals=0),
    )(me, far(hidden), far(scales), ids, slots, gate)


def by_layer_kernel(*refs):
    for r in range(LAYER):
        for i in range(1, LAYER):
            refs[LAYER + i - 1][r] = refs[r][i]


def by_layer(*blocks):
    return pl.pallas_call(
        by_layer_kernel,
        out_shape=[jax.ShapeDtypeStruct(blocks[0].shape, blocks[0].dtype)] * (LAYER - 1),
        in_specs=[VMEM] * LAYER,
        out_specs=[VMEM] * (LAYER - 1),
        compiler_params=pltpu.CompilerParams(vmem_limit_bytes=8 * MIB),
    )(*blocks)


def by_place_kernel(*refs):
    for i in range(LAYER):
        for r in range(LAYER):
            refs[LAYER + r][i] = refs[i][r]


def by_place(*blocks):
    return pl.pallas_call(
        by_place_kernel,
        out_shape=[jax.ShapeDtypeStruct(blocks[0].shape, blocks[0].dtype)] * LAYER,
        in_specs=[VMEM] * LAYER,
        out_specs=[VMEM] * LAYER,
        compiler_params=pltpu.CompilerParams(vmem_limit_bytes=8 * MIB),
    )(*blocks)


def assemble_kernel(me_ref, *refs):
    *block_refs, out_ref = refs
    here, away = block_refs[:LAYER], block_refs[LAYER:]
    for r in range(LAYER):
        for i in range(LAYER):
            out_ref[me_ref[0] ^ (LAYER * i + r)] = away[i - 1][r] if away and i else here[r][i]


def assemble(me, here, away=()):
    return pl.pallas_call(
        assemble_kernel,
        out_shape=jax.ShapeDtypeStruct((LAYER * LAYER,) + here[0].shape[1:], here[0].dtype),
        in_specs=[SMEM] + [VMEM] * (LAYER + len(away)),
        out_specs=VMEM,
        compiler_params=pltpu.CompilerParams(vmem_limit_bytes=8 * MIB),
    )(me, *here, *away)


def attention_kernel(me_ref, codes_ref, rows_ref, *refs):
    *slot_outs, attended_out, framed, attended, codes = refs
    sources, count, triple = rows_ref.shape
    width = triple // 3
    places = count // FRAMES
    piece = 2 * places
    order = frame_order(2 * count, False)
    for c in range(sources // 2):
        rows = rows_ref[2 * c : 2 * c + 2].reshape(2 * count, triple)
        rows = jnp.dot(order, rows, preferred_element_type=jnp.float32)
        framed[:, c * piece : (c + 1) * piece, :] = rows.astype(jnp.bfloat16).reshape(FRAMES, piece, triple)
    queries = framed[:, :, :width]
    keys = framed[:, :, width : 2 * width]
    values = framed[:, :, 2 * width :]
    scores = lax.dot_general(
        queries, keys, (((2,), (2,)), ((0,), (0,))), preferred_element_type=jnp.float32
    ) * width ** (-0.5)
    exponent = jnp.exp(scores - jnp.max(scores, axis=-1, keepdims=True))
    weights = (exponent / jnp.sum(exponent, axis=-1, keepdims=True)).astype(jnp.bfloat16)
    result = lax.dot_general(weights, values, (((2,), (1,)), ((0,), (0,))), preferred_element_type=jnp.float32)
    attended[...] = result.astype(jnp.bfloat16).astype(jnp.float32)
    codes[...] = jnp.zeros_like(codes)
    for s in range(sources):
        m = me_ref[0] ^ s
        codes[s * CODE_ROWS : s * CODE_ROWS + 2, :] = codes_ref[m // LAYER, m % LAYER].astype(jnp.float32)
    by_frame = lax.dot_general(
        codes[...].astype(jnp.bfloat16),
        frame_order(count, False),
        (((1,), (1,)), ((), ())),
        preferred_element_type=jnp.float32,
    )
    slot = lax.broadcasted_iota(jnp.int32, (EXPERTS * CAP, count), 0) ^ me_ref[0] * CAP
    slot = slot.astype(jnp.float32)
    for c in range(sources // 2):
        pair = []
        for s in (2 * c, 2 * c + 1):
            code = by_frame[s * CODE_ROWS : s * CODE_ROWS + 2]
            hit = (code[0:1] == slot) | (code[1:2] == slot)
            rows = attended[:, s * places : (s + 1) * places, :].reshape(count, width).astype(jnp.bfloat16)
            attended_out[s] = rows
            rows = jnp.dot(
                jnp.where(hit, 1.0, 0.0).astype(jnp.bfloat16), rows, preferred_element_type=jnp.float32
            )
            pair.append(rows.reshape(EXPERTS // LAYER, LAYER, CAP, width))
        pair = jnp.concatenate(pair, axis=2).astype(jnp.bfloat16)
        for r, out in enumerate(slot_outs):
            out[:, 2 * c * CAP : 2 * (c + 1) * CAP, :] = pair[:, r]


def attention(me, codes, rows):
    sources, count, triple = rows.shape
    width = triple // 3
    by_frame = (FRAMES, sources * count // FRAMES)
    shapes = [(EXPERTS // LAYER, sources * CAP, width)] * LAYER + [(sources, count, width)]
    outs = pl.pallas_call(
        attention_kernel,
        out_shape=[jax.ShapeDtypeStruct(shape, jnp.bfloat16) for shape in shapes],
        in_specs=[SMEM, VMEM, VMEM],
        out_specs=[VMEM] * len(shapes),
        scratch_shapes=[
            pltpu.VMEM(by_frame + (triple,), jnp.bfloat16),
            pltpu.VMEM(by_frame + (width,), jnp.float32),
            pltpu.VMEM((sources * CODE_ROWS, count), jnp.float32),
        ],
        compiler_params=pltpu.CompilerParams(vmem_limit_bytes=20 * MIB),
        cost_estimate=pl.CostEstimate(flops=2**36, bytes_accessed=4 * MIB, transcendentals=0),
    )(me, codes, rows)
    return outs


def restore_kernel(me_ref, attended_ref, *outs):
    count = attended_ref.shape[1]
    back = frame_order(count, True)
    for m in range(LAYER * LAYER):
        rows = jnp.dot(back, attended_ref[me_ref[0] ^ m], preferred_element_type=jnp.float32)
        outs[m // LAYER][m % LAYER] = rows.astype(jnp.bfloat16)


def restore(me, attended):
    block = (LAYER,) + attended.shape[1:]
    return pl.pallas_call(
        restore_kernel,
        out_shape=[jax.ShapeDtypeStruct(block, attended.dtype)] * LAYER,
        in_specs=[SMEM, VMEM],
        out_specs=[VMEM] * LAYER,
        compiler_params=pltpu.CompilerParams(vmem_limit_bytes=16 * MIB),
        cost_estimate=pl.CostEstimate(flops=2**24, bytes_accessed=MIB, transcendentals=0),
    )(me, attended)


def normalize(resid, scales_ref):
    shifted = resid - jnp.mean(resid, axis=-1, keepdims=True)
    spread = jnp.mean(shifted * shifted, axis=-1, keepdims=True)
    normed = shifted * lax.rsqrt(spread + 1e-06) * (1.0 + scales_ref[2:3, :]) + scales_ref[1:2, :]
    return normed.astype(jnp.bfloat16)


def stage_kernel(first_hbm, after_ref, first_out, done):
    del after_ref
    copy = pltpu.make_async_copy(first_hbm.at[:, pl.ds(0, first_out.shape[1])], first_out, done)
    copy.start()
    copy.wait()


def stage(first, columns, after):
    return pl.pallas_call(
        stage_kernel,
        out_shape=pltpu.VMEM((first.shape[0], columns), first.dtype),
        in_specs=[HBM, VMEM],
        out_specs=VMEM,
        scratch_shapes=[pltpu.SemaphoreType.DMA],
        compiler_params=pltpu.CompilerParams(vmem_limit_bytes=4 * MIB),
        cost_estimate=pl.CostEstimate(flops=0, bytes_accessed=4 * first.shape[0] * columns, transcendentals=0),
    )(far(first), after)


def expert_kernel(block, arrived_ref, hidden_ref, scales_ref, first_ref, second_hbm, out_ref, rows, total, ring, done):
    blocks = first_ref.shape[1] // block
    depth = ring.shape[0]

    def fetch(step):
        place = lax.rem(step, depth)
        part = pl.ds(pl.multiple_of(step * block, block), block)
        return pltpu.make_async_copy(second_hbm.at[part], ring.at[place], done.at[place])

    for step in range(min(depth, blocks)):
        fetch(step).start()
    total[...] = jnp.zeros_like(total)
    heads, count, lanes = arrived_ref.shape
    parts = []
    for h in range(heads):
        columns = slice(h * lanes, (h + 1) * lanes)
        hidden = hidden_ref[:, h * CAP : (h + 1) * CAP, :].astype(jnp.float32)
        mixed = arrived_ref[h].astype(jnp.float32)
        parts.append(hidden.reshape(count, lanes) + scales_ref[0:1, columns] * mixed)
    rows[...] = normalize(jnp.concatenate(parts, axis=1), scales_ref)

    def work(step, _):
        columns = pl.ds(pl.multiple_of(step * block, block), block)
        inner = jnp.dot(rows[...], first_ref[:, columns], preferred_element_type=jnp.float32)
        inner = jax.nn.gelu(inner, approximate=True).astype(jnp.bfloat16)
        fetch(step).wait()
        total[...] += jnp.dot(inner, ring[lax.rem(step, depth)], preferred_element_type=jnp.float32)

        @pl.when(step + depth < blocks)
        def _():
            fetch(step + depth).start()

        return 0

    lax.fori_loop(0, blocks, work, 0)
    out_ref[...] = total[...].astype(jnp.bfloat16)


def expert(arrived, hidden_rows, scales, first, second):
    width, hidden = first.shape
    count = arrived.shape[0] * CAP
    block = math.gcd(hidden, 1024)
    depth = min(hidden // block, 3)
    return pl.pallas_call(
        functools.partial(expert_kernel, block),
        out_shape=jax.ShapeDtypeStruct((count, width), jnp.bfloat16),
        in_specs=[VMEM] * 4 + [HBM],
        out_specs=VMEM,
        scratch_shapes=[
            pltpu.VMEM((count, width), jnp.bfloat16),
            pltpu.VMEM((count, width), jnp.float32),
            pltpu.VMEM((depth, block, width), jnp.bfloat16),
            pltpu.SemaphoreType.DMA((depth,)),
        ],
        compiler_params=pltpu.CompilerParams(vmem_limit_bytes=22 * MIB),
        cost_estimate=pl.CostEstimate(
            flops=64 * count * width * hidden, bytes_accessed=2 * width * hidden, transcendentals=count * hidden
        ),
    )(held(arrived), held(hidden_rows), held(scales), held(first), far(second))


def residual_kernel(me_ref, *refs):
    *block_refs, hidden_ref, scales_ref, out_ref = refs
    lanes = block_refs[0].shape[2]
    for r in range(LAYER):
        for i in range(LAYER):
            head = me_ref[0] ^ (LAYER * i + r)
            columns = pl.ds(pl.multiple_of(head * lanes, lanes), lanes)
            mixed = block_refs[r][i].astype(jnp.float32)
            out_ref[:, columns] = hidden_ref[:, columns].astype(jnp.float32) + scales_ref[0:1, columns] * mixed


def residual(me, blocks, hidden, scales):
    return pl.pallas_call(
        residual_kernel,
        out_shape=pltpu.VMEM(hidden.shape, jnp.float32),
        in_specs=[SMEM] + [VMEM] * (LAYER + 2),
        out_specs=VMEM,
        compiler_params=pltpu.CompilerParams(vmem_limit_bytes=8 * MIB),
    )(me, *blocks, hidden, held(scales))


def combine_kernel(resid_ref, scales_ref, blending_ref, brought_ref, out_hbm, out, done):
    count, width = out.shape
    step = width // done.shape[0]
    copies = []
    for c in range(done.shape[0]):
        columns = slice(c * step, (c + 1) * step)
        mixture = jnp.dot(blending_ref[...], brought_ref[:, columns], preferred_element_type=jnp.float32)
        mixture = mixture[:count] + (mixture[count : 2 * count] + mixture[2 * count :])
        out[:, columns] = (resid_ref[:, columns] + scales_ref[3:4, columns] * mixture).astype(jnp.bfloat16)
        copies.append(pltpu.make_async_copy(out.at[:, columns], out_hbm.at[:, columns], done.at[c]))
        copies[-1].start()
    for copy in copies:
        copy.wait()


def combine(resid, scales, blending, brought):
    return pl.pallas_call(
        combine_kernel,
        out_shape=pltpu.HBM(resid.shape, jnp.bfloat16),
        in_specs=[VMEM] * 4,
        out_specs=HBM,
        scratch_shapes=[pltpu.VMEM(resid.shape, jnp.bfloat16), pltpu.SemaphoreType.DMA((4,))],
        compiler_params=pltpu.CompilerParams(vmem_limit_bytes=16 * MIB),
    )(held(resid), held(scales), held(blending), brought)


def partner(array, step):
    devices = lax.axis_size("seq")
    return lax.ppermute(array, "seq", [(i, i ^ step) for i in range(devices)])


def within_layer(stay, *blocks):
    return [stay] + [partner(block, r + 1) for r, block in enumerate(blocks)]


def across_layers(*blocks):
    return [partner(block, LAYER * (i + 1)) for i, block in enumerate(blocks)]


def gather_codes(code):
    layer = jnp.stack(within_layer(*[code] * LAYER))
    return jnp.stack([layer] + across_layers(*[layer] * (LAYER - 1)))


def direct_body(hidden_in, qkv, modulation, route_weight, expert_ids, slots, w_in, w_out):
    triple = qkv.shape[3]
    devices = lax.axis_size("seq")
    me = jnp.full((1,), lax.axis_index("seq"), jnp.int32)
    ids, slot_rows = expert_ids[0].T, slots[0].T
    owned = exchange(qkv[0])
    codes = gather_codes(slot_code(ids, slot_rows))
    scales, blending, *here = prepare(
        me, hidden_in[0], modulation[0], ids, slot_rows, route_weight[0].T, triple // 3
    )
    here = within_layer(*here)
    near, *away = by_layer(*here)
    near, *away, owned = lax.optimization_barrier((partner(near, LAYER), *away, owned))
    away = [near, partner(away[0], 2 * LAYER), partner(away[1], 3 * LAYER)]
    *slot_blocks, attended = attention(me, codes, owned)
    stay, *places = restore(me, attended)
    slots_here = within_layer(*slot_blocks)
    slots_away = by_layer(*slots_here)
    staged = stage(w_in, w_in.shape[1], slots_away[0])
    slots_away = across_layers(*slots_away)
    hidden_rows = assemble(me, here, away)
    arrived = assemble(me, slots_here, slots_away)
    *places, arrived = lax.optimization_barrier((*places, arrived))
    places = across_layers(*places)
    computed = expert(arrived, hidden_rows, scales, staged, w_out)
    *places, computed = lax.optimization_barrier((*places, computed))
    brought = exchange(computed.reshape(devices, CAP, -1))
    resid = residual(me, within_layer(*by_place(stay, *places)), hidden_in[0], scales)
    return combine(resid, scales, blending, brought.reshape(devices * CAP, -1))[None]


def attend(queries, key_rows, values):
    length, width = queries.shape
    block_rows = math.gcd(length, 512)
    stacked = queries.reshape(length // block_rows, block_rows, width)

    def scores_for(query_block):
        scores = jnp.dot(query_block, key_rows.T, preferred_element_type=jnp.float32) * width ** (-0.5)
        scores = scores - jnp.max(scores, axis=-1, keepdims=True)
        exponent = jnp.exp(scores)
        weights = (exponent / jnp.sum(exponent, axis=-1, keepdims=True)).astype(jnp.bfloat16)
        return jnp.dot(weights, values, preferred_element_type=jnp.float32).astype(jnp.bfloat16)

    return lax.map(scores_for, stacked).reshape(length, width)


def split_body(hidden_in, qkv, modulation, route_weight, expert_ids, slots, w_in, w_out):
    seq_count, head_count, row_count, triple = qkv.shape
    head_width = triple // 3
    width = head_count * head_width
    devices_seq = lax.axis_size("seq")
    frame_parts = devices_seq // (seq_count * head_count)
    local_frames = FRAMES // frame_parts
    places = row_count // FRAMES
    arranged = qkv.reshape(seq_count, head_count, places, frame_parts, local_frames, triple)
    arranged = arranged.transpose(0, 1, 3, 2, 4, 5).reshape(devices_seq, places, local_frames, triple)
    owned = lax.all_to_all(arranged, "seq", split_axis=0, concat_axis=1, tiled=True)[0]
    by_frame = owned.transpose(1, 0, 2)
    attended = lax.map(
        lambda one_frame: attend(
            one_frame[:, :head_width],
            one_frame[:, head_width : 2 * head_width],
            one_frame[:, 2 * head_width :],
        ),
        by_frame,
    )
    outgoing = attended.transpose(1, 0, 2).reshape(devices_seq, places, local_frames, head_width)
    returned = exchange(outgoing)
    mixed = returned.reshape(seq_count, head_count, frame_parts, places, local_frames, head_width)
    mixed = mixed.transpose(0, 3, 2, 4, 1, 5).reshape(seq_count, row_count, width)
    resid = hidden_in.astype(jnp.float32) + modulation[:, 0][:, None, :] * mixed.astype(jnp.float32)
    center = jnp.mean(resid, axis=-1, keepdims=True)
    shifted = resid - center
    spread = jnp.mean(shifted * shifted, axis=-1, keepdims=True)
    normed = shifted * lax.rsqrt(spread + 1e-06)
    normed = (normed * (1.0 + modulation[:, 2][:, None, :]) + modulation[:, 1][:, None, :]).astype(jnp.bfloat16)
    token_rows = normed.reshape(seq_count * row_count, width)
    choice_count = expert_ids.shape[-1]
    code = slot_code(expert_ids, slots).reshape(-1, choice_count)
    weight = route_weight.reshape(-1, choice_count)
    hits = code[:, :, None] == jnp.arange(EXPERTS * CAP, dtype=jnp.int32)
    selected_expert = jnp.sum(hits, axis=1).astype(jnp.bfloat16)
    expert_blending = jnp.sum(jnp.where(hits, weight[:, :, None], 0.0), axis=1)
    gathered = jnp.einsum(
        "tk,td->kd", selected_expert, token_rows, preferred_element_type=jnp.float32
    ).astype(jnp.bfloat16)
    shards = devices_seq // EXPERTS
    spread_rows = jnp.broadcast_to(
        gathered.reshape(EXPERTS, 1, CAP, width), (EXPERTS, shards, CAP, width)
    ).reshape(devices_seq, CAP, width)
    arrived = exchange(spread_rows)
    inner = jax.nn.gelu(
        jnp.dot(arrived.reshape(-1, width), w_in, preferred_element_type=jnp.float32), approximate=True
    ).astype(jnp.bfloat16)
    computed = jnp.dot(inner, w_out, preferred_element_type=jnp.float32).astype(jnp.bfloat16)
    brought = exchange(computed.reshape(arrived.shape))
    combined_outputs = jnp.sum(
        brought.astype(jnp.float32).reshape(EXPERTS, shards, CAP, width), axis=1
    ).reshape(EXPERTS * CAP, width)
    mixture = jnp.dot(
        expert_blending, combined_outputs, precision=lax.Precision.HIGHEST, preferred_element_type=jnp.float32
    )
    final = resid + modulation[:, 3][:, None, :] * mixture.reshape(seq_count, row_count, width)
    return final.astype(jnp.bfloat16)


def body(*arrays):
    seq_count, head_count = arrays[1].shape[:2]
    devices = lax.axis_size("seq")
    if seq_count == 1 and devices == head_count == EXPERTS == 16:
        return direct_body(*arrays)
    return split_body(*arrays)


def solution(mesh):
    in_specs = (
        P("groups", "seq", None),
        P("groups", None, "seq", None),
        P("groups", None, None),
        P("groups", "seq", None),
        P("groups", "seq", None),
        P("groups", "seq", None),
        P(None, "seq"),
        P("seq", None),
    )
    out_specs = P("groups", "seq", None)
    return jax.shard_map(body, mesh=mesh, in_specs=in_specs, out_specs=out_specs, check_vma=False)
```

```python
import functools
import math

import jax
import jax.numpy as jnp
from jax import lax
from jax.experimental import pallas as pl
from jax.experimental.pallas import tpu as pltpu
from jax.sharding import PartitionSpec as P

EXPERTS = 16
CAP = 8
FRAMES = 16
LAYER = 4
CODE_ROWS = 8
MIB = 2**20

VMEM = pl.BlockSpec(memory_space=pltpu.VMEM)
SMEM = pl.BlockSpec(memory_space=pltpu.SMEM)
HBM = pl.BlockSpec(memory_space=pltpu.HBM)


def held(array):
    return pltpu.with_memory_space_constraint(array, pltpu.VMEM)


def far(array):
    return pltpu.with_memory_space_constraint(array, pltpu.HBM)


def exchange(array):
    return lax.all_to_all(array, "seq", split_axis=0, concat_axis=0, tiled=True)


def slot_code(chosen, slot_assignment):
    return jnp.where(slot_assignment < CAP, chosen * CAP + slot_assignment, -1)


def one_hot(code, values=None, me=0):
    choices, count = code.shape
    row = lax.broadcasted_iota(jnp.int32, (EXPERTS * CAP, count), 0) ^ me * CAP
    hits = jnp.zeros(row.shape, jnp.float32)
    for i in range(choices):
        hits = hits + jnp.where(code[i : i + 1, :] == row, 1.0 if values is None else values[i : i + 1, :], 0.0)
    return hits


def frame_order(rows, transposed):
    each = rows // FRAMES
    out = lax.broadcasted_iota(jnp.int32, (rows, rows), 1 if transposed else 0)
    old = lax.broadcasted_iota(jnp.int32, (rows, rows), 0 if transposed else 1)
    return jnp.where(old == out % each * FRAMES + out // each, 1.0, 0.0).astype(jnp.bfloat16)


def prepare_kernel(
    me_ref, hidden_hbm, scales_hbm, ids_ref, slots_ref, gate_ref,
    scales_out, blending_out, *refs
):
    *outs, hidden, done = refs
    copies = [
        pltpu.make_async_copy(hidden_hbm, hidden, done.at[0]),
        pltpu.make_async_copy(scales_hbm, scales_out, done.at[1]),
    ]
    for copy in copies:
        copy.start()
    code = slot_code(ids_ref[...], slots_ref[...])
    count = code.shape[1]
    blending = one_hot(code, gate_ref[...]).T
    for i in range(3):
        part = blending.astype(jnp.bfloat16)
        blending_out[i * count : (i + 1) * count, :] = part
        blending = blending - part.astype(jnp.float32)
    chosen = one_hot(code, me=me_ref[0]).astype(jnp.bfloat16)
    for copy in copies:
        copy.wait()
    layers, packed, lanes = outs[0].shape
    rows = jnp.dot(chosen, hidden[...], preferred_element_type=jnp.float32)
    for h in range(0, packed // CAP, 2):
        pair = [
            rows[:, (h + i) * lanes : (h + i + 1) * lanes].reshape(layers, LAYER, CAP, lanes) for i in range(2)
        ]
        pair = jnp.concatenate(pair, axis=2).astype(jnp.bfloat16)
        part = slice(h * CAP, (h + 2) * CAP)
        for r, out in enumerate(outs):
            out[:, part, :] = pair[:, r]


def prepare(me, hidden, scales, ids, slots, gate, lanes):
    count, width = hidden.shape
    slot_count = EXPERTS * CAP
    layers = EXPERTS // LAYER
    block = (CAP * width // lanes, lanes)
    return pl.pallas_call(
        prepare_kernel,
        out_shape=[
            pltpu.VMEM(scales.shape, scales.dtype),
            pltpu.VMEM((3 * count, slot_count), jnp.bfloat16),
        ]
        + [jax.ShapeDtypeStruct((layers,) + block, hidden.dtype)] * LAYER,
        in_specs=[SMEM, HBM, HBM, VMEM, VMEM, VMEM],
        out_specs=[VMEM] * (2 + LAYER),
        scratch_shapes=[pltpu.VMEM(hidden.shape, hidden.dtype), pltpu.SemaphoreType.DMA((2,))],
        compiler_params=pltpu.CompilerParams(vmem_limit_bytes=16 * MIB),
        cost_estimate=pl.CostEstimate(flops=2 * slot_count * count * width, bytes_accessed=4 * MIB, transcendentals=0),
    )(me, far(hidden), far(scales), ids, slots, gate)


def by_layer_kernel(*refs):
    for r in range(LAYER):
        for i in range(1, LAYER):
            refs[LAYER + i - 1][r] = refs[r][i]


def by_layer(*blocks):
    return pl.pallas_call(
        by_layer_kernel,
        out_shape=[jax.ShapeDtypeStruct(blocks[0].shape, blocks[0].dtype)] * (LAYER - 1),
        in_specs=[VMEM] * LAYER,
        out_specs=[VMEM] * (LAYER - 1),
        compiler_params=pltpu.CompilerParams(vmem_limit_bytes=8 * MIB),
    )(*blocks)


def by_place_kernel(*refs):
    for i in range(LAYER):
        for r in range(LAYER):
            refs[LAYER + r][i] = refs[i][r]


def by_place(*blocks):
    return pl.pallas_call(
        by_place_kernel,
        out_shape=[jax.ShapeDtypeStruct(blocks[0].shape, blocks[0].dtype)] * LAYER,
        in_specs=[VMEM] * LAYER,
        out_specs=[VMEM] * LAYER,
        compiler_params=pltpu.CompilerParams(vmem_limit_bytes=8 * MIB),
    )(*blocks)


def assemble_kernel(me_ref, *refs):
    *block_refs, out_ref = refs
    here, away = block_refs[:LAYER], block_refs[LAYER:]
    for r in range(LAYER):
        for i in range(LAYER):
            out_ref[me_ref[0] ^ (LAYER * i + r)] = away[i - 1][r] if away and i else here[r][i]


def assemble(me, here, away=()):
    return pl.pallas_call(
        assemble_kernel,
        out_shape=jax.ShapeDtypeStruct((LAYER * LAYER,) + here[0].shape[1:], here[0].dtype),
        in_specs=[SMEM] + [VMEM] * (LAYER + len(away)),
        out_specs=VMEM,
        compiler_params=pltpu.CompilerParams(vmem_limit_bytes=8 * MIB),
    )(me, *here, *away)


def attention_kernel(me_ref, codes_ref, rows_ref, *refs):
    *slot_outs, attended_out, framed, attended, codes = refs
    sources, count, triple = rows_ref.shape
    width = triple // 3
    places = count // FRAMES
    piece = 2 * places
    order = frame_order(2 * count, False)
    for c in range(sources // 2):
        rows = rows_ref[2 * c : 2 * c + 2].reshape(2 * count, triple)
        rows = jnp.dot(order, rows, preferred_element_type=jnp.float32)
        framed[:, c * piece : (c + 1) * piece, :] = rows.astype(jnp.bfloat16).reshape(FRAMES, piece, triple)
    queries = framed[:, :, :width]
    keys = framed[:, :, width : 2 * width]
    values = framed[:, :, 2 * width :]
    scores = lax.dot_general(
        queries, keys, (((2,), (2,)), ((0,), (0,))), preferred_element_type=jnp.float32
    ) * width ** (-0.5)
    exponent = jnp.exp(scores - jnp.max(scores, axis=-1, keepdims=True))
    weights = (exponent / jnp.sum(exponent, axis=-1, keepdims=True)).astype(jnp.bfloat16)
    result = lax.dot_general(weights, values, (((2,), (1,)), ((0,), (0,))), preferred_element_type=jnp.float32)
    attended[...] = result.astype(jnp.bfloat16).astype(jnp.float32)
    codes[...] = jnp.zeros_like(codes)
    for s in range(sources):
        m = me_ref[0] ^ s
        codes[s * CODE_ROWS : s * CODE_ROWS + 2, :] = codes_ref[m // LAYER, m % LAYER].astype(jnp.float32)
    by_frame = lax.dot_general(
        codes[...].astype(jnp.bfloat16),
        frame_order(count, False),
        (((1,), (1,)), ((), ())),
        preferred_element_type=jnp.float32,
    )
    slot = lax.broadcasted_iota(jnp.int32, (EXPERTS * CAP, count), 0) ^ me_ref[0] * CAP
    slot = slot.astype(jnp.float32)
    for c in range(sources // 2):
        pair = []
        for s in (2 * c, 2 * c + 1):
            code = by_frame[s * CODE_ROWS : s * CODE_ROWS + 2]
            hit = (code[0:1] == slot) | (code[1:2] == slot)
            rows = attended[:, s * places : (s + 1) * places, :].reshape(count, width).astype(jnp.bfloat16)
            attended_out[s] = rows
            rows = jnp.dot(
                jnp.where(hit, 1.0, 0.0).astype(jnp.bfloat16), rows, preferred_element_type=jnp.float32
            )
            pair.append(rows.reshape(EXPERTS // LAYER, LAYER, CAP, width))
        pair = jnp.concatenate(pair, axis=2).astype(jnp.bfloat16)
        for r, out in enumerate(slot_outs):
            out[:, 2 * c * CAP : 2 * (c + 1) * CAP, :] = pair[:, r]


def attention(me, codes, rows):
    sources, count, triple = rows.shape
    width = triple // 3
    by_frame = (FRAMES, sources * count // FRAMES)
    shapes = [(EXPERTS // LAYER, sources * CAP, width)] * LAYER + [(sources, count, width)]
    outs = pl.pallas_call(
        attention_kernel,
        out_shape=[jax.ShapeDtypeStruct(shape, jnp.bfloat16) for shape in shapes],
        in_specs=[SMEM, VMEM, VMEM],
        out_specs=[VMEM] * len(shapes),
        scratch_shapes=[
            pltpu.VMEM(by_frame + (triple,), jnp.bfloat16),
            pltpu.VMEM(by_frame + (width,), jnp.float32),
            pltpu.VMEM((sources * CODE_ROWS, count), jnp.float32),
        ],
        compiler_params=pltpu.CompilerParams(vmem_limit_bytes=20 * MIB),
        cost_estimate=pl.CostEstimate(flops=2**36, bytes_accessed=4 * MIB, transcendentals=0),
    )(me, codes, rows)
    return outs


def restore_kernel(me_ref, attended_ref, *outs):
    count = attended_ref.shape[1]
    back = frame_order(count, True)
    for m in range(LAYER * LAYER):
        rows = jnp.dot(back, attended_ref[me_ref[0] ^ m], preferred_element_type=jnp.float32)
        outs[m // LAYER][m % LAYER] = rows.astype(jnp.bfloat16)


def restore(me, attended):
    block = (LAYER,) + attended.shape[1:]
    return pl.pallas_call(
        restore_kernel,
        out_shape=[jax.ShapeDtypeStruct(block, attended.dtype)] * LAYER,
        in_specs=[SMEM, VMEM],
        out_specs=[VMEM] * LAYER,
        compiler_params=pltpu.CompilerParams(vmem_limit_bytes=16 * MIB),
        cost_estimate=pl.CostEstimate(flops=2**24, bytes_accessed=MIB, transcendentals=0),
    )(me, attended)


def normalize(resid, scales_ref):
    shifted = resid - jnp.mean(resid, axis=-1, keepdims=True)
    spread = jnp.mean(shifted * shifted, axis=-1, keepdims=True)
    normed = shifted * lax.rsqrt(spread + 1e-06) * (1.0 + scales_ref[2:3, :]) + scales_ref[1:2, :]
    return normed.astype(jnp.bfloat16)


def stage_kernel(first_hbm, after_ref, first_out, done):
    del after_ref
    copy = pltpu.make_async_copy(first_hbm.at[:, pl.ds(0, first_out.shape[1])], first_out, done)
    copy.start()
    copy.wait()


def stage(first, columns, after):
    return pl.pallas_call(
        stage_kernel,
        out_shape=pltpu.VMEM((first.shape[0], columns), first.dtype),
        in_specs=[HBM, VMEM],
        out_specs=VMEM,
        scratch_shapes=[pltpu.SemaphoreType.DMA],
        compiler_params=pltpu.CompilerParams(vmem_limit_bytes=4 * MIB),
        cost_estimate=pl.CostEstimate(flops=0, bytes_accessed=4 * first.shape[0] * columns, transcendentals=0),
    )(far(first), after)


def expert_kernel(block, arrived_ref, hidden_ref, scales_ref, first_ref, second_hbm, out_ref, rows, total, ring, done):
    blocks = first_ref.shape[1] // block
    depth = ring.shape[0]

    def fetch(step):
        place = lax.rem(step, depth)
        part = pl.ds(pl.multiple_of(step * block, block), block)
        return pltpu.make_async_copy(second_hbm.at[part], ring.at[place], done.at[place])

    for step in range(min(depth, blocks)):
        fetch(step).start()
    total[...] = jnp.zeros_like(total)
    heads, count, lanes = arrived_ref.shape
    parts = []
    for h in range(heads):
        columns = slice(h * lanes, (h + 1) * lanes)
        hidden = hidden_ref[:, h * CAP : (h + 1) * CAP, :].astype(jnp.float32)
        mixed = arrived_ref[h].astype(jnp.float32)
        parts.append(hidden.reshape(count, lanes) + scales_ref[0:1, columns] * mixed)
    rows[...] = normalize(jnp.concatenate(parts, axis=1), scales_ref)

    def work(step, _):
        columns = pl.ds(pl.multiple_of(step * block, block), block)
        inner = jnp.dot(rows[...], first_ref[:, columns], preferred_element_type=jnp.float32)
        inner = jax.nn.gelu(inner, approximate=True).astype(jnp.bfloat16)
        fetch(step).wait()
        total[...] += jnp.dot(inner, ring[lax.rem(step, depth)], preferred_element_type=jnp.float32)

        @pl.when(step + depth < blocks)
        def _():
            fetch(step + depth).start()

        return 0

    lax.fori_loop(0, blocks, work, 0)
    out_ref[...] = total[...].astype(jnp.bfloat16)


def expert(arrived, hidden_rows, scales, first, second):
    width, hidden = first.shape
    count = arrived.shape[0] * CAP
    block = math.gcd(hidden, 2048)
    depth = min(hidden // block, 2)
    return pl.pallas_call(
        functools.partial(expert_kernel, block),
        out_shape=jax.ShapeDtypeStruct((count, width), jnp.bfloat16),
        in_specs=[VMEM] * 4 + [HBM],
        out_specs=VMEM,
        scratch_shapes=[
            pltpu.VMEM((count, width), jnp.bfloat16),
            pltpu.VMEM((count, width), jnp.float32),
            pltpu.VMEM((depth, block, width), jnp.bfloat16),
            pltpu.SemaphoreType.DMA((depth,)),
        ],
        compiler_params=pltpu.CompilerParams(vmem_limit_bytes=22 * MIB),
        cost_estimate=pl.CostEstimate(
            flops=64 * count * width * hidden, bytes_accessed=2 * width * hidden, transcendentals=count * hidden
        ),
    )(held(arrived), held(hidden_rows), held(scales), held(first), far(second))


def residual_kernel(me_ref, *refs):
    *block_refs, hidden_ref, scales_ref, out_ref = refs
    lanes = block_refs[0].shape[2]
    for r in range(LAYER):
        for i in range(LAYER):
            head = me_ref[0] ^ (LAYER * i + r)
            columns = pl.ds(pl.multiple_of(head * lanes, lanes), lanes)
            mixed = block_refs[r][i].astype(jnp.float32)
            out_ref[:, columns] = hidden_ref[:, columns].astype(jnp.float32) + scales_ref[0:1, columns] * mixed


def residual(me, blocks, hidden, scales):
    return pl.pallas_call(
        residual_kernel,
        out_shape=pltpu.VMEM(hidden.shape, jnp.float32),
        in_specs=[SMEM] + [VMEM] * (LAYER + 2),
        out_specs=VMEM,
        compiler_params=pltpu.CompilerParams(vmem_limit_bytes=8 * MIB),
    )(me, *blocks, hidden, held(scales))


def combine_kernel(resid_ref, scales_ref, blending_ref, brought_ref, out_hbm, out, done):
    count, width = out.shape
    step = width // done.shape[0]
    copies = []
    for c in range(done.shape[0]):
        columns = slice(c * step, (c + 1) * step)
        mixture = jnp.dot(blending_ref[...], brought_ref[:, columns], preferred_element_type=jnp.float32)
        mixture = mixture[:count] + (mixture[count : 2 * count] + mixture[2 * count :])
        out[:, columns] = (resid_ref[:, columns] + scales_ref[3:4, columns] * mixture).astype(jnp.bfloat16)
        copies.append(pltpu.make_async_copy(out.at[:, columns], out_hbm.at[:, columns], done.at[c]))
        copies[-1].start()
    for copy in copies:
        copy.wait()


def combine(resid, scales, blending, brought):
    return pl.pallas_call(
        combine_kernel,
        out_shape=pltpu.HBM(resid.shape, jnp.bfloat16),
        in_specs=[VMEM] * 4,
        out_specs=HBM,
        scratch_shapes=[pltpu.VMEM(resid.shape, jnp.bfloat16), pltpu.SemaphoreType.DMA((4,))],
        compiler_params=pltpu.CompilerParams(vmem_limit_bytes=16 * MIB),
    )(held(resid), held(scales), held(blending), brought)


def partner(array, step):
    devices = lax.axis_size("seq")
    return lax.ppermute(array, "seq", [(i, i ^ step) for i in range(devices)])


def within_layer(stay, *blocks):
    return [stay] + [partner(block, r + 1) for r, block in enumerate(blocks)]


def across_layers(*blocks):
    return [partner(block, LAYER * (i + 1)) for i, block in enumerate(blocks)]


def gather_codes(code):
    layer = jnp.stack(within_layer(*[code] * LAYER))
    return jnp.stack([layer] + across_layers(*[layer] * (LAYER - 1)))


def direct_body(hidden_in, qkv, modulation, route_weight, expert_ids, slots, w_in, w_out):
    triple = qkv.shape[3]
    devices = lax.axis_size("seq")
    me = jnp.full((1,), lax.axis_index("seq"), jnp.int32)
    ids, slot_rows = expert_ids[0].T, slots[0].T
    owned = exchange(qkv[0])
    codes = gather_codes(slot_code(ids, slot_rows))
    scales, blending, *here = prepare(
        me, hidden_in[0], modulation[0], ids, slot_rows, route_weight[0].T, triple // 3
    )
    here = within_layer(*here)
    near, *away = by_layer(*here)
    near, *away, owned = lax.optimization_barrier((partner(near, LAYER), *away, owned))
    away = [near, partner(away[0], 2 * LAYER), partner(away[1], 3 * LAYER)]
    *slot_blocks, attended = attention(me, codes, owned)
    stay, *places = restore(me, attended)
    slots_here = within_layer(*slot_blocks)
    slots_away = by_layer(*slots_here)
    staged = stage(w_in, w_in.shape[1], slots_away[0])
    slots_away = across_layers(*slots_away)
    hidden_rows = assemble(me, here, away)
    arrived = assemble(me, slots_here, slots_away)
    *places, arrived = lax.optimization_barrier((*places, arrived))
    places = across_layers(*places)
    computed = expert(arrived, hidden_rows, scales, staged, w_out)
    *places, computed = lax.optimization_barrier((*places, computed))
    brought = exchange(computed.reshape(devices, CAP, -1))
    resid = residual(me, within_layer(*by_place(stay, *places)), hidden_in[0], scales)
    return combine(resid, scales, blending, brought.reshape(devices * CAP, -1))[None]


def attend(queries, key_rows, values):
    length, width = queries.shape
    block_rows = math.gcd(length, 512)
    stacked = queries.reshape(length // block_rows, block_rows, width)

    def scores_for(query_block):
        scores = jnp.dot(query_block, key_rows.T, preferred_element_type=jnp.float32) * width ** (-0.5)
        scores = scores - jnp.max(scores, axis=-1, keepdims=True)
        exponent = jnp.exp(scores)
        weights = (exponent / jnp.sum(exponent, axis=-1, keepdims=True)).astype(jnp.bfloat16)
        return jnp.dot(weights, values, preferred_element_type=jnp.float32).astype(jnp.bfloat16)

    return lax.map(scores_for, stacked).reshape(length, width)


def split_body(hidden_in, qkv, modulation, route_weight, expert_ids, slots, w_in, w_out):
    seq_count, head_count, row_count, triple = qkv.shape
    head_width = triple // 3
    width = head_count * head_width
    devices_seq = lax.axis_size("seq")
    frame_parts = devices_seq // (seq_count * head_count)
    local_frames = FRAMES // frame_parts
    places = row_count // FRAMES
    arranged = qkv.reshape(seq_count, head_count, places, frame_parts, local_frames, triple)
    arranged = arranged.transpose(0, 1, 3, 2, 4, 5).reshape(devices_seq, places, local_frames, triple)
    owned = lax.all_to_all(arranged, "seq", split_axis=0, concat_axis=1, tiled=True)[0]
    by_frame = owned.transpose(1, 0, 2)
    attended = lax.map(
        lambda one_frame: attend(
            one_frame[:, :head_width],
            one_frame[:, head_width : 2 * head_width],
            one_frame[:, 2 * head_width :],
        ),
        by_frame,
    )
    outgoing = attended.transpose(1, 0, 2).reshape(devices_seq, places, local_frames, head_width)
    returned = exchange(outgoing)
    mixed = returned.reshape(seq_count, head_count, frame_parts, places, local_frames, head_width)
    mixed = mixed.transpose(0, 3, 2, 4, 1, 5).reshape(seq_count, row_count, width)
    resid = hidden_in.astype(jnp.float32) + modulation[:, 0][:, None, :] * mixed.astype(jnp.float32)
    center = jnp.mean(resid, axis=-1, keepdims=True)
    shifted = resid - center
    spread = jnp.mean(shifted * shifted, axis=-1, keepdims=True)
    normed = shifted * lax.rsqrt(spread + 1e-06)
    normed = (normed * (1.0 + modulation[:, 2][:, None, :]) + modulation[:, 1][:, None, :]).astype(jnp.bfloat16)
    token_rows = normed.reshape(seq_count * row_count, width)
    choice_count = expert_ids.shape[-1]
    code = slot_code(expert_ids, slots).reshape(-1, choice_count)
    weight = route_weight.reshape(-1, choice_count)
    hits = code[:, :, None] == jnp.arange(EXPERTS * CAP, dtype=jnp.int32)
    selected_expert = jnp.sum(hits, axis=1).astype(jnp.bfloat16)
    expert_blending = jnp.sum(jnp.where(hits, weight[:, :, None], 0.0), axis=1)
    gathered = jnp.einsum(
        "tk,td->kd", selected_expert, token_rows, preferred_element_type=jnp.float32
    ).astype(jnp.bfloat16)
    shards = devices_seq // EXPERTS
    spread_rows = jnp.broadcast_to(
        gathered.reshape(EXPERTS, 1, CAP, width), (EXPERTS, shards, CAP, width)
    ).reshape(devices_seq, CAP, width)
    arrived = exchange(spread_rows)
    inner = jax.nn.gelu(
        jnp.dot(arrived.reshape(-1, width), w_in, preferred_element_type=jnp.float32), approximate=True
    ).astype(jnp.bfloat16)
    computed = jnp.dot(inner, w_out, preferred_element_type=jnp.float32).astype(jnp.bfloat16)
    brought = exchange(computed.reshape(arrived.shape))
    combined_outputs = jnp.sum(
        brought.astype(jnp.float32).reshape(EXPERTS, shards, CAP, width), axis=1
    ).reshape(EXPERTS * CAP, width)
    mixture = jnp.dot(
        expert_blending, combined_outputs, precision=lax.Precision.HIGHEST, preferred_element_type=jnp.float32
    )
    final = resid + modulation[:, 3][:, None, :] * mixture.reshape(seq_count, row_count, width)
    return final.astype(jnp.bfloat16)


def body(*arrays):
    seq_count, head_count = arrays[1].shape[:2]
    devices = lax.axis_size("seq")
    if seq_count == 1 and devices == head_count == EXPERTS == 16:
        return direct_body(*arrays)
    return split_body(*arrays)


def solution(mesh):
    in_specs = (
        P("groups", "seq", None),
        P("groups", None, "seq", None),
        P("groups", None, None),
        P("groups", "seq", None),
        P("groups", "seq", None),
        P("groups", "seq", None),
        P(None, "seq"),
        P("seq", None),
    )
    out_specs = P("groups", "seq", None)
    return jax.shard_map(body, mesh=mesh, in_specs=in_specs, out_specs=out_specs, check_vma=False)
```
